32 devices in a mesh: dp: 8 (over z, core), cls: 4 (over y, x).
Axes of the slice: x: 2, y: 2, z: 4, core: 2. Of those that a mesh axis runs over, the one named last changes fastest.
Arguments:
- attended: bfloat16 [27648, 1024], P(('dp', 'cls')), may hold values from -6 to 6
- stream: bfloat16 [27648, 1024], P(('dp', 'cls')), may hold values from -6 to 6
- out_proj: bfloat16 [1024, 1024], P('dp'), may hold values from -0.1875 to 0.1875
- norm_gain: float32 [1024], replicated, may hold values from 0.25 to 1.75
- norm_shift: float32 [1024], replicated, may hold values from -0.75 to 0.75
- head_proj: bfloat16 [1024, 512], P('dp'), may hold values from -0.1875 to 0.1875
- class_weight: bfloat16 [4096, 512], P('cls'), may hold values from -6 to 6
- block_ids: int32 [8, 4, 3], P('dp', 'cls'), may hold values from 0 to 7, as said below
- block_count: int32 [8, 4], P('dp', 'cls'), may hold values from 1 to 3, as said below
- labels: int32 [192], P('dp'), may hold values from 0 to 4095, as said below
Outputs:
- sample_loss: float32 [192], P(('dp', 'cls'))
- embed_grad: float32 [192, 512], P(('dp', 'cls'))
- class_grad: float32 [4096, 512], P('cls', 'dp')
The draws below stay inside these ranges and needn't reach their ends.
Inputs may be any that keep to these rules, and one draw needn't show every extreme that they name: `block_ids`: within one data group and class shard the 3 block numbers are all different. `block_count`: some data group and class shard has all 3 slots live, another just one. `labels`: every image's class lies in a live slot's block of its own data group.
All inputs are finite; a program needn't handle non-finite values.
Results may differ from the reference program's by a relative error of at most 0.0028.
Values may be sent and summed in bfloat16 or wider, within the bound.
No kernel may reach another device: no remote copies, remote signals or barrier semaphores. Data moves between devices by JAX's collectives and lax.ppermute only.
A program may use at most 64 MiB of HBM per device.

```python
import math
from functools import partial
import jax
import jax.numpy as jnp
from jax import lax

D = 1024
E = 512
P_SIZE = 144
BLOCK_ROWS = 128
BLOCKS_DEV = 8
SLOTS = 3
CLS_DEV = 1024
CLASSES = 4096
GROUP = 24
IMAGES = 192
N_DP = 8
N_CLS = 4


def sample_plan(key):
    subkeys = jax.random.split(jax.random.fold_in(key, 11), 7)
    scores = jax.random.randint(subkeys[0], (N_DP, N_CLS, BLOCKS_DEV), 0, 1 << 20) * BLOCKS_DEV + jnp.arange(BLOCKS_DEV, dtype=jnp.int32)
    ranking = jnp.argsort(scores, axis=-1, stable=True)
    slot_ids = ranking[:, :, :SLOTS].astype(jnp.int32)
    pairs = N_DP * N_CLS
    counts = jax.random.randint(subkeys[1], (pairs,), 1, SLOTS + 1)
    full_at = jax.random.randint(subkeys[2], (), 0, pairs)
    single_at = (full_at + 1 + jax.random.randint(subkeys[3], (), 0, pairs - 1)) % pairs
    counts = counts.at[full_at].set(SLOTS).at[single_at].set(1).reshape(N_DP, N_CLS).astype(jnp.int32)
    group_of = jnp.arange(IMAGES, dtype=jnp.int32) // GROUP
    shard_pick = jax.random.randint(subkeys[4], (IMAGES,), 0, N_CLS)
    slot_pick = jax.random.randint(subkeys[5], (IMAGES,), 0, 1 << 20) % counts[group_of, shard_pick]
    row_pick = jax.random.randint(subkeys[6], (IMAGES,), 0, BLOCK_ROWS)
    block_pick = slot_ids[group_of, shard_pick, slot_pick]
    target = shard_pick * (BLOCKS_DEV * BLOCK_ROWS) + block_pick * BLOCK_ROWS + row_pick
    return (slot_ids, counts, target.astype(jnp.int32))


def draw_block_ids(key, part):
    return sample_plan(key)[0]


def draw_block_count(key, part):
    return sample_plan(key)[1]


def draw_labels(key, part):
    return sample_plan(key)[2]


def levels(stream_key, shape, pieces, low, largest):
    def one(axis_at, shards_of):
        draws = jax.random.uniform(jax.random.fold_in(jax.random.fold_in(stream_key, 6), axis_at), (shards_of,), jnp.float32, low / len(pieces), largest / len(pieces))
        return jnp.repeat(jnp.exp(draws), shape[axis_at] // shards_of).reshape((-1,) + (1,) * (len(shape) - axis_at - 1))

    level = one(*pieces[0])
    for cut in pieces[1:]:
        level = level * one(*cut)
    return level


def noise(stream_key, extent, width, bound, cuts=(), kind=jnp.bfloat16):
    drawn = width * jax.random.normal(stream_key, extent, jnp.float32)
    if cuts:
        drawn = drawn * levels(stream_key, extent, cuts, -0.22, 0.18)
    return jnp.clip(drawn, -bound, bound).astype(kind)


def setup_inputs(seed: int = 0) -> dict:
    arg_keys = jax.random.split(jax.random.key(seed), 11)
    attended = noise(arg_keys[0], (IMAGES * P_SIZE, D), 1.0, 6.0, ((0, 32),))
    stream = noise(arg_keys[1], (IMAGES * P_SIZE, D), 1.0, 6.0, ((0, 32),))
    out_proj = noise(arg_keys[2], (D, D), D ** -0.5, 0.1875, ((0, 8),))
    norm_gain = jnp.clip(1.0 + 0.15 * jax.random.normal(arg_keys[3], (D,), jnp.float32), 0.25, 1.75)
    norm_shift = noise(arg_keys[4], (D,), 0.05, 0.75, (), jnp.float32)
    head_proj = noise(arg_keys[5], (D, E), D ** -0.5, 0.1875, ((0, 8),))
    class_weight = noise(arg_keys[6], (CLASSES, E), 1.0, 6.0, ((0, 4),))
    block_ids = draw_block_ids(jax.random.fold_in(arg_keys[10], 71), 0)
    block_count = draw_block_count(jax.random.fold_in(arg_keys[10], 71), 0)
    labels = draw_labels(jax.random.fold_in(arg_keys[10], 71), 0)
    return dict(attended=attended, stream=stream, out_proj=out_proj, norm_gain=norm_gain, norm_shift=norm_shift, head_proj=head_proj, class_weight=class_weight, block_ids=block_ids, block_count=block_count, labels=labels)


LOGIT_SCALE = 64.0
ANGLE_MARGIN = 0.5
NORM_EPSILON = 1e-06

def pool_group(group_tokens, out_proj, norm_gain, norm_shift):
    attended, stream = group_tokens
    mixed = stream.astype(jnp.float32) + jnp.dot(attended, out_proj, preferred_element_type=jnp.float32)
    token_mean = lax.optimization_barrier(jnp.mean(mixed, axis=1, keepdims=True))
    centred = mixed - token_mean
    variance = lax.optimization_barrier(jnp.mean(centred * centred, axis=1, keepdims=True))
    normed = norm_gain * centred / jnp.sqrt(variance + NORM_EPSILON) + norm_shift
    return lax.optimization_barrier(jnp.mean(normed.reshape(GROUP, P_SIZE, D), axis=1)).astype(jnp.bfloat16)

def reference(attended, stream, out_proj, norm_gain, norm_shift, head_proj, class_weight, block_ids, block_count, labels):
    pooled = lax.map(partial(pool_group, out_proj=out_proj, norm_gain=norm_gain, norm_shift=norm_shift), (attended.reshape(N_DP, GROUP * P_SIZE, D), stream.reshape(N_DP, GROUP * P_SIZE, D)))
    pooled = pooled.reshape(IMAGES, D)
    embedding = jnp.dot(pooled, head_proj, preferred_element_type=jnp.float32)
    embed_norm = jnp.sqrt(lax.optimization_barrier(jnp.sum(embedding * embedding, axis=1)) + NORM_EPSILON)
    unit_embed = embedding / embed_norm[:, None]
    weight_blocks = class_weight.reshape(N_CLS, BLOCKS_DEV, BLOCK_ROWS, E)
    shard_range = jnp.arange(N_CLS, dtype=jnp.int32)
    slot_range = jnp.arange(SLOTS, dtype=jnp.int32)
    row_range = jnp.arange(BLOCK_ROWS, dtype=jnp.int32)
    block_range = jnp.arange(BLOCKS_DEV, dtype=jnp.int32)

    def step_group(dense_total, group_data):
        unit_group, norm_group, slot_ids, live_count, group_labels = group_data
        picked = weight_blocks[shard_range[:, None], slot_ids].astype(jnp.float32).reshape(-1, E)
        weight_norm = jnp.sqrt(lax.optimization_barrier(jnp.sum(picked * picked, axis=1)) + NORM_EPSILON)
        unit_weight = picked / weight_norm[:, None]
        cosine = jnp.dot(unit_group, unit_weight.T, precision=lax.Precision.HIGHEST, preferred_element_type=jnp.float32)
        slot_live = slot_range[None, :] < live_count[:, None]
        live_mask = jnp.broadcast_to(slot_live[:, :, None], (N_CLS, SLOTS, BLOCK_ROWS)).reshape(-1)
        column_class = (shard_range[:, None, None] * CLS_DEV + slot_ids[:, :, None] * BLOCK_ROWS + row_range[None, None, :]).reshape(-1)
        target_mask = (column_class[None, :] == group_labels[:, None]) & live_mask[None, :]
        target_cos = cosine * math.cos(ANGLE_MARGIN) - jnp.sqrt(1.0 - cosine * cosine) * math.sin(ANGLE_MARGIN)
        logits = LOGIT_SCALE * jnp.where(target_mask, target_cos, cosine)
        exponent = jnp.where(live_mask[None, :], jnp.exp(logits - LOGIT_SCALE), 0.0)
        denominator = lax.optimization_barrier(jnp.sum(exponent, axis=1))
        target_logit = lax.optimization_barrier(jnp.sum(jnp.where(target_mask, logits, 0.0), axis=1))
        sample_loss = jnp.log(denominator) + LOGIT_SCALE - target_logit
        target_float = target_mask.astype(jnp.float32)
        cos_grad = LOGIT_SCALE * (exponent / denominator[:, None] - target_float)
        unit_grad = jnp.dot(cos_grad, unit_weight, precision=lax.Precision.HIGHEST, preferred_element_type=jnp.float32)
        embed_grad = (unit_grad - unit_group * lax.optimization_barrier(jnp.sum(unit_group * unit_grad, axis=1, keepdims=True))) / norm_group[:, None]
        weight_unit_grad = jnp.dot(cos_grad.T, unit_group, precision=lax.Precision.HIGHEST, preferred_element_type=jnp.float32)
        weight_grad = (weight_unit_grad - unit_weight * lax.optimization_barrier(jnp.sum(unit_weight * weight_unit_grad, axis=1, keepdims=True))) / weight_norm[:, None]
        placement = ((block_range[None, :, None] == slot_ids[:, None, :]) & slot_live[:, None, :]).astype(jnp.float32)
        dense_grad = jnp.einsum('cbk,ckx->cbx', placement, weight_grad.reshape(N_CLS, SLOTS, BLOCK_ROWS * E), precision=lax.Precision.HIGHEST)
        return (dense_total + dense_grad, (sample_loss, embed_grad))
    initial = jnp.zeros((N_CLS, BLOCKS_DEV, BLOCK_ROWS * E), jnp.float32)
    dense_total, outputs = lax.scan(step_group, initial, (unit_embed.reshape(N_DP, GROUP, E), embed_norm.reshape(N_DP, GROUP), block_ids, block_count, labels.reshape(N_DP, GROUP)))
    sample_loss, embed_grad = outputs
    return (sample_loss.reshape(IMAGES), embed_grad.reshape(IMAGES, E), dense_total.reshape(CLASSES, E))
```

```python
import math

import jax
import jax.numpy as jnp
from jax import lax
from jax.experimental import pallas as pl
from jax.experimental.pallas import tpu as pltpu
from jax.sharding import PartitionSpec as P

P_SIZE = 144
BLOCK_ROWS = 128
CORES = 2

LOGIT_SCALE = 64.0
ANGLE_MARGIN = 0.5
NORM_EPSILON = 1e-06
HIGHEST = lax.Precision.HIGHEST


def z_swap(value, step):
    count = lax.axis_size("dp")
    return lax.ppermute(value, "dp", [(i, i ^ (step * CORES)) for i in range(count)])


def core_swap(value):
    count = lax.axis_size("dp")
    return lax.ppermute(value, "dp", [(i, i ^ 1) for i in range(count)])


def plane_swap(value, step):
    count = lax.axis_size("cls")
    return lax.ppermute(value, "cls", [(i, i ^ step) for i in range(count)])


def pool_kernel(part_ref, att_ref, own_ref, other_ref, gain_ref, shift_ref, out_ref, mixed_ref, pooled_ref):
    tokens, width = part_ref.shape
    images = tokens // P_SIZE
    depth = own_ref.shape[0]
    per = 3 if images % 3 == 0 else 1
    chunk = per * P_SIZE
    for start in range(0, tokens, chunk):
        rows = pl.ds(start, chunk)
        mixed_ref[rows, :] = (
            part_ref[rows, :]
            + jnp.dot(att_ref[rows, pl.ds(0, depth)], own_ref[...], preferred_element_type=jnp.float32)
            + jnp.dot(att_ref[rows, pl.ds(depth, depth)], other_ref[...], preferred_element_type=jnp.float32)
        )
    step = 24
    for image in range(images):
        total = jnp.zeros((8, width), jnp.float32)
        for r in range(0, P_SIZE, step):
            x = mixed_ref[pl.ds(image * P_SIZE + r, step), :]
            centred = x - jnp.mean(x, axis=1, keepdims=True)
            variance = jnp.mean(centred * centred, axis=1, keepdims=True)
            scaled = centred * lax.rsqrt(variance + NORM_EPSILON)
            total = total + jnp.sum(scaled.reshape(step // 8, 8, width), axis=0)
        mean = jnp.sum(total, axis=0, keepdims=True) * (1.0 / P_SIZE)
        pooled_ref[pl.ds(image, 1), :] = gain_ref[...] * mean + shift_ref[...]
    out_ref[...] = pooled_ref[...].astype(out_ref.dtype)


def pool_tokens(part, att, own, other, gain, shift):
    tokens, width = part.shape
    images = tokens // P_SIZE
    vmem = pl.BlockSpec(memory_space=pltpu.VMEM)
    return pl.pallas_call(
        pool_kernel,
        out_shape=jax.ShapeDtypeStruct((images, width), jnp.bfloat16),
        in_specs=[vmem] * 6,
        out_specs=vmem,
        scratch_shapes=[
            pltpu.VMEM((tokens, width), jnp.float32),
            pltpu.VMEM((images, width), jnp.float32),
        ],
        compiler_params=pltpu.CompilerParams(vmem_limit_bytes=24 * 1024 * 1024),
        cost_estimate=pl.CostEstimate(
            flops=4 * tokens * width * own.shape[0], bytes_accessed=8 * tokens * width, transcendentals=tokens
        ),
    )(part, att, own, other, gain.reshape(1, width), shift.reshape(1, width))


def per_device(
    attended,
    stream,
    out_proj,
    norm_gain,
    norm_shift,
    head_proj,
    class_weight,
    block_ids,
    block_count,
    labels,
):
    n_dp, n_cls = lax.axis_size("dp"), lax.axis_size("cls")
    n_z = n_dp // CORES
    dp, cls = lax.axis_index("dp"), lax.axis_index("cls")
    z, core = dp // CORES, dp % CORES
    tokens, width = attended.shape
    images = tokens // P_SIZE
    rows = out_proj.shape[0]
    slice_rows = rows // n_cls

    own_slice = lax.dynamic_slice_in_dim(out_proj, cls * slice_rows, slice_rows, 0)
    far = [z_swap(own_slice, step) for step in range(n_z - 1, 1, -1)]
    near = z_swap(out_proj, 1)
    far = jnp.stack(far)
    whole_far = jnp.zeros((n_z - 2, n_cls, slice_rows, width), out_proj.dtype)
    whole_far = lax.dynamic_update_slice_in_dim(whole_far, far[:, None], cls, 1)
    for step in range(n_cls - 1, 0, -1):
        whole_far = lax.dynamic_update_slice_in_dim(
            whole_far, plane_swap(far, step)[:, None], cls ^ step, 1
        )
    whole_far = whole_far.reshape((n_z - 2) * rows, width)
    two = jnp.concatenate([out_proj, near], axis=0)
    other_two = core_swap(two)
    other_far = core_swap(whole_far)

    def columns_of(steps):
        taken = []
        for side in (core, 1 - core):
            for step in steps:
                at = ((z ^ step) * CORES + side) * rows
                taken.append(lax.dynamic_slice_in_dim(attended, at, rows, 1))
        return jnp.concatenate(taken, axis=1)

    part = stream.astype(jnp.float32) + jnp.dot(
        columns_of((0, 1)), jnp.concatenate([two, other_two], axis=0), preferred_element_type=jnp.float32
    )
    att_far = columns_of(range(n_z - 1, 1, -1))
    pooled = pool_tokens(part, att_far, whole_far, other_far, norm_gain, norm_shift)

    heads = jnp.stack([head_proj] + [z_swap(head_proj, step) for step in range(1, n_z)])
    other_heads = core_swap(heads)
    head = jnp.zeros((n_z, CORES) + head_proj.shape, head_proj.dtype)
    for step in range(n_z):
        for k, source in ((0, heads), (1, other_heads)):
            head = lax.dynamic_update_slice(
                head, source[step][None, None], (z ^ step, core ^ k, 0, 0)
            )
    head = head.reshape(n_dp * head_proj.shape[0], -1)

    own_labels = labels.reshape(n_cls, images)
    label_rows = jnp.concatenate(
        [lax.dynamic_slice_in_dim(own_labels, cls ^ step, 1, 0) for step in range(n_cls)], axis=0
    ).reshape(-1)
    facts = jnp.concatenate(
        [block_ids[0, 0], block_count[0], label_rows // BLOCK_ROWS, label_rows % BLOCK_ROWS]
    ).astype(jnp.bfloat16)
    n_facts = facts.shape[0]
    facts = jnp.pad(facts, (0, width - n_facts))[None]
    group = jnp.concatenate(
        [pooled] + [plane_swap(pooled, step) for step in range(1, n_cls)] + [facts], axis=0
    )
    groups = jnp.stack([group] + [z_swap(group, step) for step in range(1, n_z)])
    groups = jnp.concatenate([groups, core_swap(groups)], axis=0)
    size = n_cls * images
    pooled_all = groups[:, :size].reshape(n_dp * size, width)
    slots = block_ids.shape[2]
    facts_all = groups[:, size, :n_facts].astype(jnp.int32)
    ids = facts_all[:, :slots]
    count = facts_all[:, slots]
    label_block = facts_all[:, slots + 1 : slots + 1 + size].reshape(-1)
    label_row = facts_all[:, slots + 1 + size :].reshape(-1)

    classes, embed = class_weight.shape
    weight = class_weight.astype(jnp.float32)
    weight_norm = jnp.sqrt(jnp.sum(weight * weight, axis=1) + NORM_EPSILON)
    unit_weight = weight / weight_norm[:, None]

    embedding = jnp.dot(pooled_all, head, preferred_element_type=jnp.float32)
    embed_norm = jnp.sqrt(jnp.sum(embedding * embedding, axis=1) + NORM_EPSILON)
    unit_embed = embedding / embed_norm[:, None]
    cosine = jnp.dot(unit_embed, unit_weight.T, precision=HIGHEST, preferred_element_type=jnp.float32)

    blocks = classes // BLOCK_ROWS
    block_range = jnp.arange(blocks, dtype=jnp.int32)
    live = jnp.any(
        (ids[:, :, None] == block_range) & (jnp.arange(slots)[None, :, None] < count[:, None, None]), axis=1
    )
    live = jnp.broadcast_to(live[:, None, :, None], (n_dp, size, blocks, BLOCK_ROWS)).reshape(-1, classes)
    class_index = jnp.arange(classes, dtype=jnp.int32) + cls * classes
    label = label_block * BLOCK_ROWS + label_row
    target = (class_index[None, :] == label[:, None]) & live
    target_cos = cosine * math.cos(ANGLE_MARGIN) - jnp.sqrt(1.0 - cosine * cosine) * math.sin(ANGLE_MARGIN)
    logits = LOGIT_SCALE * jnp.where(target, target_cos, cosine)
    exponent = jnp.where(live, jnp.exp(logits), 0.0)
    denom_part = jnp.sum(exponent, axis=1)
    target_part = jnp.sum(jnp.where(target, logits, 0.0), axis=1)
    target_float = target.astype(jnp.float32)
    both = jnp.concatenate([exponent[:size], target_float[:size]], axis=0)
    sums = jnp.dot(both, unit_weight, precision=HIGHEST, preferred_element_type=jnp.float32)
    sums = sums.reshape(2, n_cls, images, embed)
    denom_part = denom_part.reshape(n_dp, n_cls, images)
    target_part = target_part[:size].reshape(n_cls, images)

    def packed(step):
        order = [k ^ step for k in range(n_cls)]
        denoms = denom_part[:, jnp.array(order)].reshape(-1)
        tail = jnp.concatenate([denoms, target_part[step]])
        lines = -(-tail.shape[0] // embed)
        tail = jnp.pad(tail, (0, lines * embed - tail.shape[0])).reshape(lines, embed)
        return jnp.concatenate([sums[0, step], sums[1, step], tail], axis=0)

    total = packed(0)
    for step in range(1, n_cls):
        total = total + plane_swap(packed(step), step)
    weighted, picked = total[:images], total[images : 2 * images]
    tail = total[2 * images :].reshape(-1)
    denominator = tail[: n_dp * size]
    target_logit = tail[n_dp * size : n_dp * size + images]
    own_denominator = denominator[:images]
    sample_loss = jnp.log(own_denominator) - target_logit
    unit_grad = LOGIT_SCALE * (weighted / own_denominator[:, None] - picked)
    unit_own = unit_embed[:images]
    embed_grad = (
        unit_grad - unit_own * jnp.sum(unit_own * unit_grad, axis=1, keepdims=True)
    ) / embed_norm[:images, None]

    cos_grad = LOGIT_SCALE * (exponent / denominator[:, None] - target_float)
    share = embed // n_dp
    unit_share = lax.dynamic_slice_in_dim(unit_embed, dp * share, share, 1)
    weight_share = lax.dynamic_slice_in_dim(unit_weight, dp * share, share, 1)
    along = jnp.sum(cos_grad * cosine, axis=0)
    grad = lax.dot_general(
        unit_share, cos_grad, (((0,), (0,)), ((), ())), precision=HIGHEST, preferred_element_type=jnp.float32
    )
    class_grad = ((grad - weight_share.T * along[None, :]) / weight_norm[None, :]).T
    return (sample_loss, embed_grad, class_grad)


def solution(mesh):
    placed = (
        P(("dp", "cls"), None),
        P(("dp", "cls"), None),
        P("dp", None),
        P(),
        P(),
        P("dp", None),
        P("cls", None),
        P("dp", "cls", None),
        P("dp", "cls"),
        P("dp"),
    )
    return jax.shard_map(
        per_device,
        mesh=mesh,
        in_specs=placed,
        out_specs=(P(("dp", "cls")), P(("dp", "cls"), None), P("cls", "dp")),
        check_vma=False,
    )
```

```python
import functools
import math

import jax
import jax.numpy as jnp
from jax import lax
from jax.experimental import pallas as pl
from jax.experimental.pallas import tpu as pltpu
from jax.sharding import PartitionSpec as P

P_SIZE = 144
BLOCK_ROWS = 128
CORES = 2

LOGIT_SCALE = 64.0
ANGLE_MARGIN = 0.5
NORM_EPSILON = 1e-06


def z_swap(value, step):
    count = lax.axis_size("dp")
    return lax.ppermute(value, "dp", [(i, i ^ (step * CORES)) for i in range(count)])


def core_swap(value):
    count = lax.axis_size("dp")
    return lax.ppermute(value, "dp", [(i, i ^ 1) for i in range(count)])


def plane_swap(value, step):
    count = lax.axis_size("cls")
    return lax.ppermute(value, "cls", [(i, i ^ step) for i in range(count)])


def pool_kernel(part_ref, att_ref, own_ref, other_ref, gain_ref, shift_ref, out_ref, mixed_ref, pooled_ref):
    tokens, width = part_ref.shape
    images = tokens // P_SIZE
    depth = own_ref.shape[0]
    per = 3 if images % 3 == 0 else 1
    chunk = per * P_SIZE
    for start in range(0, tokens, chunk):
        rows = pl.ds(start, chunk)
        mixed_ref[rows, :] = (
            part_ref[rows, :]
            + jnp.dot(att_ref[rows, pl.ds(0, depth)], own_ref[...], preferred_element_type=jnp.float32)
            + jnp.dot(att_ref[rows, pl.ds(depth, depth)], other_ref[...], preferred_element_type=jnp.float32)
        )
    step = 24
    for image in range(images):
        total = jnp.zeros((8, width), jnp.float32)
        for r in range(0, P_SIZE, step):
            x = mixed_ref[pl.ds(image * P_SIZE + r, step), :]
            centred = x - jnp.mean(x, axis=1, keepdims=True)
            variance = jnp.mean(centred * centred, axis=1, keepdims=True)
            scaled = centred * lax.rsqrt(variance + NORM_EPSILON)
            total = total + jnp.sum(scaled.reshape(step // 8, 8, width), axis=0)
        mean = jnp.sum(total, axis=0, keepdims=True) * (1.0 / P_SIZE)
        pooled_ref[pl.ds(image, 1), :] = gain_ref[...] * mean + shift_ref[...]
    out_ref[...] = pooled_ref[...].astype(out_ref.dtype)


def pool_tokens(part, att, own, other, gain, shift):
    tokens, width = part.shape
    images = tokens // P_SIZE
    vmem = pl.BlockSpec(memory_space=pltpu.VMEM)
    return pl.pallas_call(
        pool_kernel,
        out_shape=jax.ShapeDtypeStruct((images, width), jnp.bfloat16),
        in_specs=[vmem] * 6,
        out_specs=vmem,
        scratch_shapes=[
            pltpu.VMEM((tokens, width), jnp.float32),
            pltpu.VMEM((images, width), jnp.float32),
        ],
        compiler_params=pltpu.CompilerParams(vmem_limit_bytes=24 * 1024 * 1024),
        cost_estimate=pl.CostEstimate(
            flops=4 * tokens * width * own.shape[0], bytes_accessed=8 * tokens * width, transcendentals=tokens
        ),
    )(part, att, own, other, gain.reshape(1, width), shift.reshape(1, width))


def split(value):
    high = value.astype(jnp.bfloat16)
    return high, (value - high.astype(jnp.float32)).astype(jnp.bfloat16)


def as_row(column):
    return jnp.broadcast_to(column, (column.shape[0], 128)).T[0:1]


def class_kernel(own, pooled_ref, head_ref, code_ref, weight_ref, scale_ref,
                 exp_ref, cos_ref, unit_ref, sums_ref, denom_ref):
    images = pooled_ref.shape[0]
    classes, embed = weight_ref.shape
    embedding = jnp.dot(pooled_ref[...], head_ref[...], preferred_element_type=jnp.float32)
    norm = jnp.sqrt(jnp.sum(embedding * embedding, axis=1, keepdims=True) + NORM_EPSILON)
    unit = embedding * (1.0 / norm)
    unit_ref[:, :embed] = unit
    unit_ref[:, embed:] = jnp.broadcast_to(norm, (images, 128))
    terms = jnp.concatenate(split(unit), axis=0)
    denom = jnp.zeros((images, 128), jnp.float32)
    picked = jnp.zeros((own, 128), jnp.float32)
    wide = 256
    for start in range(0, classes, wide):
        cols = pl.ds(start, wide)
        both = lax.dot_general(
            terms, weight_ref[cols, :], (((1,), (1,)), ((), ())), preferred_element_type=jnp.float32
        )
        cosine = (both[:images] + both[images:]) * scale_ref[:, cols]
        cos_ref[:, cols] = cosine
        code = code_ref[:, cols]
        target = code > 1.5
        sine = jnp.sqrt(jnp.maximum(1.0 - cosine * cosine, 0.0))
        margin = cosine * math.cos(ANGLE_MARGIN) - sine * math.sin(ANGLE_MARGIN)
        logits = LOGIT_SCALE * jnp.where(target, margin, cosine)
        exponent = jnp.where(code > 0.5, jnp.exp(logits), 0.0)
        exp_ref[:, cols] = exponent
        labelled = jnp.where(target, logits, 0.0)[:own]
        for k in range(0, wide, 128):
            denom = denom + exponent[:, k : k + 128]
            picked = picked + labelled[:, k : k + 128]
    denom = jnp.sum(denom, axis=1, keepdims=True)
    denom_ref[...] = as_row(denom)
    scale = scale_ref[...]
    weighted = split(exp_ref[:own, :] * scale)
    chosen = split(jnp.where(code_ref[:own, :] > 1.5, scale, 0.0))
    sums = jnp.dot(
        jnp.concatenate(weighted + chosen, axis=0), weight_ref[...], preferred_element_type=jnp.float32
    )
    sums_ref[:, :embed] = sums[:own] + sums[own : 2 * own]
    sums_ref[:, embed : 2 * embed] = sums[2 * own : 3 * own] + sums[3 * own :]
    sums_ref[:, 2 * embed : 2 * embed + 128] = jnp.broadcast_to(denom[:own], (own, 128))
    sums_ref[:, 2 * embed + 128 :] = jnp.broadcast_to(jnp.sum(picked, axis=1, keepdims=True), (own, 128))


def class_parts(own, pooled, head, code, weight, scale):
    images = pooled.shape[0]
    classes, embed = weight.shape
    vmem = pl.BlockSpec(memory_space=pltpu.VMEM)
    f32 = jnp.float32
    return pl.pallas_call(
        functools.partial(class_kernel, own),
        out_shape=(
            jax.ShapeDtypeStruct((images, classes), f32),
            jax.ShapeDtypeStruct((images, classes), f32),
            jax.ShapeDtypeStruct((images, embed + 128), f32),
            jax.ShapeDtypeStruct((own, 2 * embed + 256), f32),
            jax.ShapeDtypeStruct((1, images), f32),
        ),
        in_specs=[vmem] * 5,
        out_specs=(vmem,) * 5,
        compiler_params=pltpu.CompilerParams(vmem_limit_bytes=24 * 1024 * 1024),
        cost_estimate=pl.CostEstimate(
            flops=6 * images * embed * classes, bytes_accessed=16 * images * classes, transcendentals=images * classes
        ),
    )(pooled, head, code, weight, scale)


def grad_kernel(denom_ref, exp_ref, cos_ref, code_ref, unit_ref, weight_ref, scale_ref, grad_ref):
    ratio = LOGIT_SCALE / denom_ref[...]
    unit = unit_ref[...]
    share, images = unit.shape
    left = jnp.concatenate(split(unit * ratio), axis=0)
    exponent = exp_ref[...]
    high, low = split(exponent)
    dot = functools.partial(jnp.dot, preferred_element_type=jnp.float32)
    first = dot(left, high)
    grad = first[:share] + first[share:] + dot(left[:share], low)
    target = code_ref[...] > 1.5
    second = dot(jnp.concatenate(split(unit * LOGIT_SCALE), axis=0), jnp.where(target, 1.0, 0.0).astype(jnp.bfloat16))
    grad = grad - second[:share] - second[share:]
    cosine = cos_ref[...]
    column = jnp.broadcast_to(ratio, (128, images)).T
    along = jnp.zeros((1, cosine.shape[1]), jnp.float32)
    weighted = exponent * column[:, 0:1] - jnp.where(target, LOGIT_SCALE, 0.0)
    along = jnp.sum(weighted * cosine, axis=0, keepdims=True)
    scale = scale_ref[...]
    grad_ref[...] = (grad - weight_ref[...] * (along * scale)) * scale


def class_grad_part(denom, exponent, cosine, code, unit_share, weight_share, scale):
    share, images = unit_share.shape
    classes = exponent.shape[1]
    vmem = pl.BlockSpec(memory_space=pltpu.VMEM)
    return pl.pallas_call(
        grad_kernel,
        out_shape=jax.ShapeDtypeStruct((share, classes), jnp.float32),
        in_specs=[vmem] * 7,
        out_specs=vmem,
        compiler_params=pltpu.CompilerParams(vmem_limit_bytes=24 * 1024 * 1024),
        cost_estimate=pl.CostEstimate(
            flops=10 * images * share * classes, bytes_accessed=12 * images * classes, transcendentals=0
        ),
    )(denom, exponent, cosine, code, unit_share, weight_share, scale)


def per_device(
    attended,
    stream,
    out_proj,
    norm_gain,
    norm_shift,
    head_proj,
    class_weight,
    block_ids,
    block_count,
    labels,
):
    n_dp, n_cls = lax.axis_size("dp"), lax.axis_size("cls")
    n_z = n_dp // CORES
    dp, cls = lax.axis_index("dp"), lax.axis_index("cls")
    z, core = dp // CORES, dp % CORES
    tokens, width = attended.shape
    images = tokens // P_SIZE
    rows = out_proj.shape[0]
    slice_rows = rows // n_cls

    size = n_cls * images
    slots = block_ids.shape[2]
    classes, embed = class_weight.shape

    facts = jnp.concatenate(
        [block_ids[0, 0], block_count[0], labels // BLOCK_ROWS, labels % BLOCK_ROWS]
    ).astype(jnp.bfloat16)
    n_facts = facts.shape[0]
    facts = jnp.pad(facts, (0, 16 * embed - n_facts)).reshape(16, embed)

    own_slice = lax.dynamic_slice_in_dim(out_proj, cls * slice_rows, slice_rows, 0)
    far = [z_swap(own_slice, step) for step in range(n_z - 1, 1, -1)]
    far = jnp.stack(far)
    late_out, far_first = lax.optimization_barrier((out_proj, own_slice))
    near = z_swap(late_out, 1)
    two = jnp.concatenate([out_proj, near], axis=0)
    attended, stream, class_weight, head_proj, far = lax.optimization_barrier(
        (attended, stream, class_weight, head_proj, far)
    )
    from_plane = [plane_swap(far, step) for step in range(n_cls - 1, 0, -1)]
    whole_far = jnp.zeros((n_z - 2, n_cls, slice_rows, width), out_proj.dtype)
    whole_far = lax.dynamic_update_slice_in_dim(whole_far, far[:, None], cls, 1)
    for step, got in zip(range(n_cls - 1, 0, -1), from_plane):
        whole_far = lax.dynamic_update_slice_in_dim(whole_far, got[:, None], cls ^ step, 1)
    whole_far = whole_far.reshape((n_z - 2) * rows, width)
    other_two = core_swap(two)
    other_far = core_swap(whole_far)

    def columns_of(steps):
        taken = []
        for side in (core, 1 - core):
            for step in steps:
                at = ((z ^ step) * CORES + side) * rows
                taken.append(lax.dynamic_slice_in_dim(attended, at, rows, 1))
        return jnp.concatenate(taken, axis=1)

    part = stream.astype(jnp.float32) + jnp.dot(
        columns_of((0, 1)), jnp.concatenate([two, other_two], axis=0), preferred_element_type=jnp.float32
    )
    att_far = columns_of(range(n_z - 1, 1, -1))

    pooled = pool_tokens(part, att_far, whole_far, other_far, norm_gain, norm_shift)

    head_rows = head_proj.shape[0]
    head_own = jnp.concatenate([head_proj, facts], axis=0)
    heads = jnp.stack([head_own] + [z_swap(head_own, step) for step in range(1, n_z)])
    other_heads = core_swap(heads)
    head = jnp.zeros((n_z, CORES, head_rows, embed), head_proj.dtype)
    for step in range(n_z):
        for k, source in ((0, heads), (1, other_heads)):
            head = lax.dynamic_update_slice(
                head, source[step, :head_rows][None, None], (z ^ step, core ^ k, 0, 0)
            )
    head = head.reshape(n_dp * head_rows, embed)
    all_facts = jnp.concatenate([heads[:, head_rows:], other_heads[:, head_rows:]], axis=0)
    all_facts = all_facts.reshape(n_dp, 16 * embed)[:, :n_facts].astype(jnp.int32)

    block_of = jnp.arange(classes, dtype=jnp.int32) // BLOCK_ROWS
    code = jnp.zeros((n_dp, 1, classes), jnp.float32)
    for slot in range(slots):
        used = (all_facts[:, slot, None] == block_of) & (slot < all_facts[:, slots, None])
        code = jnp.where(used[:, None, :], 1.0, code)
    label = all_facts[:, slots + 1 : slots + 1 + size] * BLOCK_ROWS + all_facts[:, slots + 1 + size :]
    hit = (label - cls * classes)[:, :, None] == jnp.arange(classes, dtype=jnp.int32)
    code = jnp.where(hit & (code > 0.5), 2.0, jnp.broadcast_to(code, hit.shape)).reshape(-1, classes)

    scale = lax.rsqrt(
        jnp.sum(jnp.square(class_weight.astype(jnp.float32)), axis=1) + NORM_EPSILON
    )[None, :]
    share = embed // n_dp
    weight_share = lax.dynamic_slice_in_dim(class_weight, dp * share, share, 1).T.astype(jnp.float32)

    group = jnp.zeros((n_cls, images, width), pooled.dtype)
    for step, got in [(0, pooled)] + [(step, plane_swap(pooled, step)) for step in range(n_cls - 1, 0, -1)]:
        group = lax.dynamic_update_slice_in_dim(group, got[None], cls ^ step, 0)
    group = group.reshape(size, width)
    groups = jnp.stack([group] + [z_swap(group, step) for step in range(1, n_z)])
    groups = jnp.concatenate([groups, core_swap(groups)], axis=0)
    pooled_all = groups.reshape(n_dp * size, width)

    piece = size * max(1, min(n_dp, 192 // size))
    own = -(-size // 16) * 16
    parts = [
        class_parts(own, pooled_all[at : at + piece], head, code[at : at + piece], class_weight, scale)
        for at in range(0, n_dp * size, piece)
    ]
    denoms = jnp.concatenate([p[4] for p in parts], axis=1)
    sums = parts[0][3]
    lines = -(-denoms.shape[1] // sums.shape[1])
    denoms = jnp.pad(denoms, ((0, 0), (0, lines * sums.shape[1] - denoms.shape[1]))).reshape(lines, -1)

    def packed(step):
        return jnp.concatenate(
            [lax.dynamic_slice_in_dim(sums, (cls ^ step) * images, images, 0), denoms], axis=0
        )

    total = packed(0)
    for step in range(n_cls - 1, 0, -1):
        total = total + plane_swap(packed(step), step)
    denominator = total[images:].reshape(1, -1)[:, : n_dp * size]
    class_grad = jnp.zeros((share, classes), jnp.float32)
    for k, (exponent, cosine, unit, _, _) in enumerate(parts):
        at = k * piece
        unit_share = lax.dynamic_slice_in_dim(unit, dp * share, share, 1).T
        grad = class_grad_part(
            denominator[:, at : at + piece], exponent, cosine, code[at : at + piece], unit_share, weight_share, scale
        )
        class_grad = grad if k == 0 else class_grad + grad

    weighted, picked = total[:images, :embed], total[:images, embed : 2 * embed]
    own_denominator = total[:images, 2 * embed]
    target_logit = total[:images, 2 * embed + 128]
    sample_loss = jnp.log(own_denominator) - target_logit
    unit_grad = LOGIT_SCALE * (weighted / own_denominator[:, None] - picked)
    own_unit = lax.dynamic_slice_in_dim(parts[0][2], cls * images, images, 0)
    unit_own, norm_own = own_unit[:, :embed], own_unit[:, embed : embed + 1]
    embed_grad = (
        unit_grad - unit_own * jnp.sum(unit_own * unit_grad, axis=1, keepdims=True)
    ) / norm_own
    return (sample_loss, embed_grad, class_grad.T)


def solution(mesh):
    placed = (
        P(("dp", "cls"), None),
        P(("dp", "cls"), None),
        P("dp", None),
        P(),
        P(),
        P("dp", None),
        P("cls", None),
        P("dp", "cls", None),
        P("dp", "cls"),
        P("dp"),
    )
    return jax.shard_map(
        per_device,
        mesh=mesh,
        in_specs=placed,
        out_specs=(P(("dp", "cls")), P(("dp", "cls"), None), P("cls", "dp")),
        check_vma=False,
    )
```

```python
import functools
import math

import jax
import jax.numpy as jnp
from jax import lax
from jax.experimental import pallas as pl
from jax.experimental.pallas import tpu as pltpu
from jax.sharding import PartitionSpec as P

P_SIZE = 144
BLOCK_ROWS = 128
CORES = 2

LOGIT_SCALE = 64.0
ANGLE_MARGIN = 0.5
NORM_EPSILON = 1e-06


def z_swap(value, step):
    count = lax.axis_size("dp")
    return lax.ppermute(value, "dp", [(i, i ^ (step * CORES)) for i in range(count)])


def core_swap(value):
    count = lax.axis_size("dp")
    return lax.ppermute(value, "dp", [(i, i ^ 1) for i in range(count)])


def plane_swap(value, step):
    count = lax.axis_size("cls")
    return lax.ppermute(value, "cls", [(i, i ^ step) for i in range(count)])


def pool_kernel(att_ref, stream_ref, own_ref, near_ref, own_other_ref, near_other_ref, far_ref, far_other_ref,
                gain_ref, shift_ref, out_ref, weight_ref, mixed_ref, pooled_ref):
    tokens, width = stream_ref.shape
    images = tokens // P_SIZE
    rows = own_ref.shape[0]
    n_cls, n_far, slice_rows, _ = far_ref.shape
    dp, cls = lax.axis_index("dp"), lax.axis_index("cls")
    z, core = dp // CORES, dp % CORES

    def place(shard, start, value):
        at = pl.multiple_of(shard * rows + start, slice_rows)
        weight_ref[pl.ds(at, value.shape[0]), :] = value

    for side, own, near, far in (
        (core, own_ref, near_ref, far_ref), (1 - core, own_other_ref, near_other_ref, far_other_ref)
    ):
        place(z * CORES + side, 0, own[...])
        place((z ^ 1) * CORES + side, 0, near[...])
        for k in range(n_far):
            for step in range(n_cls):
                start = (cls ^ step) * slice_rows if n_cls > 1 else 0
                place((z ^ (k + 2)) * CORES + side, start, far[step, k])
    per = 3 if images % 3 == 0 else 1
    chunk = per * P_SIZE
    for start in range(0, tokens, chunk):
        here = pl.ds(start, chunk)
        mixed_ref[here, :] = stream_ref[here, :].astype(jnp.float32) + jnp.dot(
            att_ref[here, :], weight_ref[...], preferred_element_type=jnp.float32
        )
    step = 24
    for image in range(images):
        total = jnp.zeros((8, width), jnp.float32)
        for r in range(0, P_SIZE, step):
            x = mixed_ref[pl.ds(image * P_SIZE + r, step), :]
            centred = x - jnp.mean(x, axis=1, keepdims=True)
            variance = jnp.mean(centred * centred, axis=1, keepdims=True)
            scaled = centred * lax.rsqrt(variance + NORM_EPSILON)
            total = total + jnp.sum(scaled.reshape(step // 8, 8, width), axis=0)
        mean = jnp.sum(total, axis=0, keepdims=True) * (1.0 / P_SIZE)
        pooled_ref[pl.ds(image, 1), :] = gain_ref[...] * mean + shift_ref[...]
    if images < pooled_ref.shape[0]:
        pooled_ref[images:, :] = jnp.zeros((pooled_ref.shape[0] - images, width), jnp.float32)
    out_ref[...] = pooled_ref[...].astype(out_ref.dtype)


def padded(images):
    return -(-images // 8) * 8


def in_vmem(kernel, outs, scratch, mib, flops, operands):
    vmem = pl.BlockSpec(memory_space=pltpu.VMEM)
    moved = sum(math.prod(x.shape) * x.dtype.itemsize for x in list(operands) + list(outs))
    return pl.pallas_call(
        kernel,
        out_shape=tuple(outs),
        in_specs=[vmem] * len(operands),
        out_specs=(vmem,) * len(outs),
        scratch_shapes=scratch,
        compiler_params=pltpu.CompilerParams(vmem_limit_bytes=mib * 1024 * 1024),
        cost_estimate=pl.CostEstimate(flops=flops, bytes_accessed=moved, transcendentals=0),
    )(*operands)


def f32(*shape):
    return jax.ShapeDtypeStruct(shape, jnp.float32)


def pool_tokens(*operands):
    tokens, width = operands[0].shape
    lines = padded(tokens // P_SIZE)
    return in_vmem(
        pool_kernel,
        [jax.ShapeDtypeStruct((lines, width), jnp.bfloat16)],
        [
            pltpu.VMEM((width, width), jnp.bfloat16),
            pltpu.VMEM((tokens, width), jnp.float32),
            pltpu.VMEM((lines, width), jnp.float32),
        ],
        12,
        2 * tokens * width * width,
        operands,
    )[0]


def split(value):
    high = value.astype(jnp.bfloat16)
    return high, (value - high.astype(jnp.float32)).astype(jnp.bfloat16)


def as_row(column):
    return jnp.broadcast_to(column, (column.shape[0], 128)).T[0:1]


def over_lanes(left, right):
    return lax.dot_general(left, right, (((1,), (1,)), ((), ())), preferred_element_type=jnp.float32)


def one_hot(rows, columns, at):
    row = lax.broadcasted_iota(jnp.int32, (rows, columns), 0)
    column = lax.broadcasted_iota(jnp.int32, (rows, columns), 1)
    return jnp.where(column == at(row), 1.0, 0.0).astype(jnp.bfloat16)


def masks(image_ref, start, wide):
    images = image_ref.shape[0]
    label, bits = image_ref[:, 0:1], image_ref[:, 1:2]
    live = [
        jnp.broadcast_to((bits & (1 << (k // BLOCK_ROWS))) != 0, (images, BLOCK_ROWS))
        for k in range(start, start + wide, BLOCK_ROWS)
    ]
    live = jnp.concatenate(live, axis=1)
    column = lax.broadcasted_iota(jnp.int32, (images, wide), 1) + start
    return live, live & (column == label)


def class_kernel(own, pooled_ref, head_ref, other_ref, image_ref, weight_ref, scale_ref,
                 exp_ref, cos_ref, unit_ref, sums_ref, denom_ref, whole_ref, chosen_ref, group_ref):
    images = pooled_ref.shape[0]
    classes, embed = weight_ref.shape
    n_z = head_ref.shape[0]
    n_cls = sums_ref.shape[0]
    rows = pooled_ref.shape[1] // (CORES * n_z)
    dp, cls = lax.axis_index("dp"), lax.axis_index("cls")
    z, core = dp // CORES, dp % CORES
    for k in range(n_z):
        for side, source in ((core, head_ref), (1 - core, other_ref)):
            at = pl.multiple_of(((z ^ k) * CORES + side) * rows, rows)
            whole_ref[pl.ds(at, rows), :] = source[k, :rows, :]
    embedding = jnp.dot(pooled_ref[...], whole_ref[...], preferred_element_type=jnp.float32)
    norm = jnp.sqrt(jnp.sum(embedding * embedding, axis=1, keepdims=True) + NORM_EPSILON)
    unit = embedding * (1.0 / norm)
    unit_ref[:, :embed] = unit
    unit_ref[:, embed:] = jnp.broadcast_to(norm, (images, 128))
    terms = jnp.concatenate(split(unit), axis=0)
    denom = jnp.zeros((images, 128), jnp.float32)
    picked = jnp.zeros((own, 128), jnp.float32)
    wide = 256
    for start in range(0, classes, wide):
        cols = pl.ds(start, wide)
        both = over_lanes(terms, weight_ref[cols, :])
        cosine = (both[:images] + both[images:]) * scale_ref[:, cols]
        cos_ref[:, cols] = cosine
        live, target = masks(image_ref, start, wide)
        sine = jnp.sqrt(jnp.maximum(1.0 - cosine * cosine, 0.0))
        margin = cosine * math.cos(ANGLE_MARGIN) - sine * math.sin(ANGLE_MARGIN)
        logits = LOGIT_SCALE * jnp.where(target, margin, cosine)
        exponent = jnp.where(live, jnp.exp(logits), 0.0)
        exp_ref[:, cols] = exponent
        labelled = jnp.where(target, logits, 0.0)[:own]
        chosen_ref[:, cols] = jnp.where(target[:own], scale_ref[:, cols], 0.0)
        for k in range(0, wide, 128):
            denom = denom + exponent[:, k : k + 128]
            picked = picked + labelled[:, k : k + 128]
    denom = jnp.sum(denom, axis=1, keepdims=True)
    denom_ref[...] = as_row(denom)
    weighted = split(exp_ref[:own, :] * scale_ref[...])
    chosen = split(chosen_ref[...])
    sums = jnp.dot(
        jnp.concatenate(weighted + chosen, axis=0), weight_ref[...], preferred_element_type=jnp.float32
    )
    sums = jnp.concatenate(
        [
            sums[:own] + sums[own : 2 * own],
            sums[2 * own : 3 * own] + sums[3 * own :],
            jnp.broadcast_to(denom[:own], (own, 128)),
            jnp.broadcast_to(jnp.sum(picked, axis=1, keepdims=True), (own, 128)),
        ],
        axis=1,
    )
    group_ref[...] = sums
    lines = sums_ref.shape[1]
    for step in range(n_cls):
        at = pl.multiple_of((cls ^ step) * lines, lines)
        sums_ref[step] = group_ref[pl.ds(at, lines), :]


def class_parts(own, n_cls, *operands):
    pooled, head, _, _, weight, _ = operands
    images, width = pooled.shape
    classes, embed = weight.shape
    return in_vmem(
        functools.partial(class_kernel, own),
        [
            f32(images, classes),
            f32(images, classes),
            f32(images, embed + 128),
            f32(n_cls, own // n_cls, 2 * embed + 256),
            f32(1, images),
        ],
        [
            pltpu.VMEM((width, embed), jnp.bfloat16),
            pltpu.VMEM((own, classes), jnp.float32),
            pltpu.VMEM((own, 2 * embed + 256), jnp.float32),
        ],
        6,
        6 * images * embed * classes,
        operands,
    )


def grad_kernel(share, total_ref, denom_ref, exp_ref, cos_ref, unit_ref, image_ref, weight_ref, scale_ref,
                grad_ref, loss_ref, embed_ref):
    images, classes = exp_ref.shape
    embed = weight_ref.shape[1]
    at = lax.axis_index("dp") * share
    block = pl.ds(pl.multiple_of(at // 128 * 128, 128), 128)
    take = one_hot(share, 128, lambda row: row + at % 128)
    high, low = split(unit_ref[:, block])
    unit = over_lanes(take, high) + over_lanes(take, low)
    weight = over_lanes(take, weight_ref[:, block])
    denom = denom_ref[...]
    ratio = jnp.where(denom > 0.0, LOGIT_SCALE / denom, 0.0)
    left = jnp.concatenate(split(unit * ratio), axis=0)
    marked = jnp.concatenate(split(unit * LOGIT_SCALE), axis=0)
    column = jnp.broadcast_to(ratio, (128, images)).T[:, 0:1]
    dot = functools.partial(jnp.dot, preferred_element_type=jnp.float32)
    wide = 256
    for start in range(0, classes, wide):
        cols = pl.ds(start, wide)
        exponent = exp_ref[:, cols]
        _, target = masks(image_ref, start, wide)
        high, low = split(exponent)
        first = dot(left, high)
        second = dot(marked, jnp.where(target, 1.0, 0.0).astype(jnp.bfloat16))
        grad = first[:share] + first[share:] + dot(left[:share], low) - second[:share] - second[share:]
        weighted = exponent * column - jnp.where(target, LOGIT_SCALE, 0.0)
        along = jnp.sum(weighted * cos_ref[:, cols], axis=0, keepdims=True)
        scale = scale_ref[:, cols]
        grad_ref[:, cols] = (grad - weight[:, start : start + wide] * (along * scale)) * scale

    lines = padded(embed_ref.shape[0])
    own = unit_ref[pl.ds(pl.multiple_of(lax.axis_index("cls") * lines, lines), lines), :][: embed_ref.shape[0]]
    total = total_ref[: embed_ref.shape[0], :]
    weighted, picked = total[:, :embed], total[:, embed : 2 * embed]
    own_denom, target_logit = total[:, 2 * embed : 2 * embed + 1], total[:, 2 * embed + 128 : 2 * embed + 129]
    loss = jnp.broadcast_to(jnp.log(own_denom) - target_logit, (loss_ref.shape[1], 128))
    loss = jnp.concatenate([loss, jnp.zeros((128 - loss_ref.shape[1], 128), jnp.float32)], axis=0)
    loss_ref[...] = loss.T[0:1, : loss_ref.shape[1]]
    unit_grad = LOGIT_SCALE * (weighted / own_denom - picked)
    own_unit = own[:, :embed]
    embed_ref[...] = (
        unit_grad - own_unit * jnp.sum(own_unit * unit_grad, axis=1, keepdims=True)
    ) / own[:, embed : embed + 1]


def class_grad_part(share, own_images, *operands):
    images, classes = operands[2].shape
    embed = operands[6].shape[1]
    return in_vmem(
        functools.partial(grad_kernel, share),
        [f32(share, classes), f32(1, own_images), f32(own_images, embed)],
        [],
        6,
        10 * images * share * classes,
        operands,
    )


def per_device(
    attended,
    stream,
    out_proj,
    norm_gain,
    norm_shift,
    head_proj,
    class_weight,
    block_ids,
    block_count,
    labels,
):
    n_dp, n_cls = lax.axis_size("dp"), lax.axis_size("cls")
    n_z = n_dp // CORES
    dp, cls = lax.axis_index("dp"), lax.axis_index("cls")
    tokens, width = attended.shape
    images = tokens // P_SIZE
    size = n_cls * images
    lines = padded(images)
    group_lines = n_cls * lines
    rows = out_proj.shape[0]
    slice_rows = rows // n_cls
    slots = block_ids.shape[2]
    classes, embed = class_weight.shape

    facts = jnp.concatenate(
        [block_ids[0, 0], block_count[0], labels // BLOCK_ROWS, labels % BLOCK_ROWS]
    ).astype(jnp.bfloat16)
    n_facts = facts.shape[0]
    facts = jnp.pad(facts, (0, 16 * embed - n_facts)).reshape(16, embed)

    own_slice = lax.dynamic_slice_in_dim(out_proj, cls * slice_rows, slice_rows, 0)
    far = jnp.stack([z_swap(own_slice, step) for step in range(2, n_z)])
    near_from, _ = lax.optimization_barrier((out_proj, own_slice))
    near = z_swap(near_from, 1)
    own_other = core_swap(near_from)
    head_rows = head_proj.shape[0]
    head_own = jnp.concatenate([head_proj, facts], axis=0)
    class_weight, head_own, far = lax.optimization_barrier((class_weight, head_own, far))
    far = jnp.stack([far] + [plane_swap(far, step) for step in range(1, n_cls)])
    if slice_rows % 16:
        ordered = jnp.zeros_like(far)
        for step in range(n_cls):
            ordered = lax.dynamic_update_index_in_dim(ordered, far[step], cls ^ step, 0)
        far = ordered.transpose(1, 0, 2, 3).reshape(1, n_z - 2, rows, width)
    near_other = core_swap(near)
    far_other = core_swap(far)
    pooled = pool_tokens(
        attended, stream, out_proj, near, own_other, near_other, far, far_other,
        norm_gain.reshape(1, width), norm_shift.reshape(1, width),
    )

    heads = [z_swap(head_own, step) for step in range(1, n_z)]
    heads, pooled = lax.optimization_barrier((heads, pooled))
    heads = jnp.stack([head_own] + heads)
    other_heads = core_swap(heads)
    all_facts = jnp.concatenate([heads[:, head_rows:], other_heads[:, head_rows:]], axis=0)
    all_facts = all_facts.reshape(n_dp, 16 * embed)[:, :n_facts].astype(jnp.int32)

    bits = jnp.zeros((n_dp,), jnp.int32)
    for slot in range(slots):
        bits = bits + jnp.where(slot < all_facts[:, slots], 1 << all_facts[:, slot], 0)
    label = all_facts[:, slots + 1 : slots + 1 + size] * BLOCK_ROWS + all_facts[:, slots + 1 + size :]
    label = (label - cls * classes).reshape(n_dp, n_cls, images)
    bits = jnp.broadcast_to(bits[:, None, None], label.shape)
    image_facts = jnp.pad(jnp.stack([label, bits], axis=-1), ((0, 0), (0, 0), (0, lines - images), (0, 0)))
    image_facts = image_facts.reshape(-1, 2)

    scale = lax.rsqrt(
        jnp.sum(jnp.square(class_weight.astype(jnp.float32)), axis=1) + NORM_EPSILON
    )[None, :]

    column = jnp.stack([pooled] + [z_swap(pooled, step) for step in range(1, n_z)])
    groups = jnp.zeros((n_z, n_cls, lines, width), pooled.dtype)
    for step, got in [(0, column)] + [(step, plane_swap(column, step)) for step in range(1, n_cls)]:
        groups = lax.dynamic_update_slice_in_dim(groups, got[:, None], cls ^ step, 1)
    groups = jnp.concatenate([groups, core_swap(groups)], axis=0)
    pooled_all = groups.reshape(n_dp * group_lines, width)

    piece = group_lines * max(1, min(n_dp, 256 // group_lines))
    total_lines = n_dp * group_lines
    parts = [
        class_parts(
            group_lines, n_cls, pooled_all[at : at + piece], heads, other_heads, image_facts[at : at + piece],
            class_weight, scale,
        )
        for at in range(0, total_lines, piece)
    ]
    denoms = jnp.concatenate([p[4] for p in parts], axis=1)
    sums = parts[0][3]
    extra = -(-total_lines // sums.shape[2])
    denoms = jnp.pad(denoms, ((0, 0), (0, extra * sums.shape[2] - total_lines))).reshape(extra, -1)

    def packed(step):
        return jnp.concatenate([sums[step, :images], denoms], axis=0)

    total = packed(0)
    for step in range(n_cls - 1, 0, -1):
        total = total + plane_swap(packed(step), step)
    denominator = total[images:].reshape(1, -1)[:, :total_lines]
    share = embed // n_dp
    for k, (exponent, cosine, unit, _, _) in enumerate(parts):
        at = k * piece
        grad, loss, embed_part = class_grad_part(
            share, images, total, denominator[:, at : at + piece], exponent, cosine, unit,
            image_facts[at : at + piece], class_weight, scale,
        )
        if k == 0:
            class_grad, sample_loss, embed_grad = grad, loss, embed_part
        else:
            class_grad = class_grad + grad
    return (sample_loss.reshape(images), embed_grad, class_grad.T)


def solution(mesh):
    placed = (
        P(("dp", "cls"), None),
        P(("dp", "cls"), None),
        P("dp", None),
        P(),
        P(),
        P("dp", None),
        P("cls", None),
        P("dp", "cls", None),
        P("dp", "cls"),
        P("dp"),
    )
    return jax.shard_map(
        per_device,
        mesh=mesh,
        in_specs=placed,
        out_specs=(P(("dp", "cls")), P(("dp", "cls"), None), P("cls", "dp")),
        check_vma=False,
    )
```

```python
import functools
import math

import jax
import jax.numpy as jnp
from jax import lax
from jax.experimental import pallas as pl
from jax.experimental.pallas import tpu as pltpu
from jax.sharding import PartitionSpec as P

P_SIZE = 144
BLOCK_ROWS = 128
CORES = 2
FACT_ROWS = 16

LOGIT_SCALE = 64.0
ANGLE_MARGIN = 0.5
NORM_EPSILON = 1e-06


def z_swap(value, step):
    count = lax.axis_size("dp")
    return lax.ppermute(value, "dp", [(i, i ^ (step * CORES)) for i in range(count)])


def core_swap(value):
    count = lax.axis_size("dp")
    return lax.ppermute(value, "dp", [(i, i ^ 1) for i in range(count)])


def half_swap(value):
    n_dp, n_cls = lax.axis_size("dp"), lax.axis_size("cls")
    pairs = [(dp * n_cls + c, dp * n_cls + (c ^ (1 << dp % CORES))) for dp in range(n_dp) for c in range(n_cls)]
    return lax.ppermute(value, ("dp", "cls"), pairs)


def plane_swap(value, step):
    count = lax.axis_size("cls")
    return lax.ppermute(value, "cls", [(i, i ^ step) for i in range(count)])


def pool_kernel(att_ref, stream_ref, own_ref, near_ref, own_other_ref, near_other_ref, far_ref, far_other_ref, gain_ref, shift_ref,
                out_ref, weight_ref, mixed_ref, pooled_ref):
    tokens, width = stream_ref.shape
    images = tokens // P_SIZE
    chunk = mixed_ref.shape[0]
    pieces = range(0, tokens, chunk)
    n_cls, n_far, slice_rows, _ = far_ref.shape
    rows = n_cls * slice_rows
    dp, cls = lax.axis_index("dp"), lax.axis_index("cls")
    z, core = dp // CORES, dp % CORES

    def place(shard, start, value):
        at = pl.multiple_of(shard * rows + start, slice_rows)
        weight_ref[pl.ds(at, value.shape[0]), :] = value

    for side, own, near, far in (
        (core, own_ref, near_ref, far_ref), (1 - core, own_other_ref, near_other_ref, far_other_ref)
    ):
        place(z * CORES + side, 0, own[...])
        place((z ^ 1) * CORES + side, 0, near[...])
        for k in range(n_far):
            for step in range(n_cls):
                start = (cls ^ step) * slice_rows if n_cls > 1 else 0
                place((z ^ (k + 2)) * CORES + side, start, far[step, k])
    step = 24
    for k, start in enumerate(pieces):
        mixed_ref[...] = jnp.dot(
            att_ref[pl.ds(start, chunk), :], weight_ref[...], preferred_element_type=jnp.float32
        )
        for image in range(chunk // P_SIZE):
            total = jnp.zeros((8, width), jnp.float32)
            for r in range(0, P_SIZE, step):
                at = image * P_SIZE + r
                x = mixed_ref[pl.ds(at, step), :] + stream_ref[pl.ds(start + at, step), :].astype(jnp.float32)
                centred = x - jnp.mean(x, axis=1, keepdims=True)
                variance = jnp.mean(centred * centred, axis=1, keepdims=True)
                scaled = centred * lax.rsqrt(variance + NORM_EPSILON)
                total = total + jnp.sum(scaled.reshape(step // 8, 8, width), axis=0)
            mean = jnp.sum(total, axis=0, keepdims=True) * (1.0 / P_SIZE)
            pooled_ref[pl.ds(start // P_SIZE + image, 1), :] = gain_ref[...] * mean + shift_ref[...]
    if images < pooled_ref.shape[0]:
        pooled_ref[images:, :] = jnp.zeros((pooled_ref.shape[0] - images, width), jnp.float32)
    out_ref[...] = pooled_ref[...].astype(out_ref.dtype)


def padded(images):
    return -(-images // 8) * 8


def after(value, *others):
    anywhere = pl.BlockSpec(memory_space=pl.ANY)
    return pl.pallas_call(
        lambda *refs: None,
        out_shape=jax.ShapeDtypeStruct(value.shape, value.dtype),
        in_specs=[anywhere] * (1 + len(others)),
        out_specs=anywhere,
        input_output_aliases={0: 0},
        compiler_params=pltpu.CompilerParams(vmem_limit_bytes=1024 * 1024),
    )(value, *others)


def in_vmem(kernel, outs, scratch, mib, flops, operands, in_hbm=0):
    vmem = pl.BlockSpec(memory_space=pltpu.VMEM)
    moved = sum(math.prod(x.shape) * x.dtype.itemsize for x in list(operands) + list(outs))
    return pl.pallas_call(
        kernel,
        out_shape=tuple(outs),
        in_specs=[pl.BlockSpec(memory_space=pl.ANY)] * in_hbm + [vmem] * (len(operands) - in_hbm),
        out_specs=(vmem,) * len(outs),
        scratch_shapes=scratch,
        compiler_params=pltpu.CompilerParams(vmem_limit_bytes=mib * 1024 * 1024),
        cost_estimate=pl.CostEstimate(flops=flops, bytes_accessed=moved, transcendentals=0),
    )(*operands)


def f32(*shape):
    return jax.ShapeDtypeStruct(shape, jnp.float32)


def pool_tokens(*operands):
    tokens, width = operands[0].shape
    images = tokens // P_SIZE
    lines = padded(images)
    chunk = (3 if images % 3 == 0 else 1) * P_SIZE
    return in_vmem(
        pool_kernel,
        [jax.ShapeDtypeStruct((lines, width), jnp.bfloat16)],
        [
            pltpu.VMEM((width, width), jnp.bfloat16),
            pltpu.VMEM((chunk, width), jnp.float32),
            pltpu.VMEM((lines, width), jnp.float32),
        ],
        12,
        2 * tokens * width * width,
        operands,
    )[0]


def split(value):
    high = value.astype(jnp.bfloat16)
    return high, (value - high.astype(jnp.float32)).astype(jnp.bfloat16)


def as_row(column):
    return jnp.broadcast_to(column, (column.shape[0], 128)).T[0:1]


def over_lanes(left, right):
    return lax.dot_general(left, right, (((1,), (1,)), ((), ())), preferred_element_type=jnp.float32)


def one_hot(rows, columns, at):
    row = lax.broadcasted_iota(jnp.int32, (rows, columns), 0)
    column = lax.broadcasted_iota(jnp.int32, (rows, columns), 1)
    return jnp.where(column == at(row), 1.0, 0.0).astype(jnp.bfloat16)


def masks(image_ref, start, wide):
    images = image_ref.shape[0]
    label, bits = image_ref[:, 0:1], image_ref[:, 1:2]
    live = [
        jnp.broadcast_to((bits & (1 << (k // BLOCK_ROWS))) != 0, (images, BLOCK_ROWS))
        for k in range(start, start + wide, BLOCK_ROWS)
    ]
    live = jnp.concatenate(live, axis=1)
    column = lax.broadcasted_iota(jnp.int32, (images, wide), 1) + start
    return live, live & (column == label)


def class_kernel(own, head_rows, slots, group_images, base, pooled_ref, head_ref, other_ref, weight_ref, scale_ref,
                 exp_ref, cos_ref, unit_ref, sums_ref, denom_ref, image_ref, whole_ref, chosen_ref, group_ref):
    images = pooled_ref.shape[0]
    classes, embed = weight_ref.shape
    n_cls = sums_ref.shape[0]
    dp, cls = lax.axis_index("dp"), lax.axis_index("cls")
    z, core = dp // CORES, dp % CORES
    n_z = pooled_ref.shape[1] // (CORES * head_rows)
    half = head_rows // 2
    block = half + FACT_ROWS
    size = group_images * n_cls
    lines = own // n_cls
    fact_lanes = -(-(slots + 1 + 2 * size) // 128) * 128
    row = lax.broadcasted_iota(jnp.int32, (own, fact_lanes), 0)
    lane = lax.broadcasted_iota(jnp.int32, (own, fact_lanes), 1)
    image = slots + 1 + row // lines * group_images + row % lines
    block_at = (lane == image) & (row % lines < group_images)
    row_at = (lane == image + size) & (row % lines < group_images)
    for side, source in ((core, head_ref), (1 - core, other_ref)):
        mine = (cls >> side) & 1
        for k in range(n_z):
            for part, which in ((0, mine), (1, 1 - mine)):
                at = pl.multiple_of(((z ^ k) * CORES + side) * head_rows + which * half, half)
                whole_ref[pl.ds(at, half), :] = source[pl.ds((part * n_z + k) * block, half), :]
    for which, source in enumerate((head_ref, other_ref)):
        for k in range(n_z):
            at = (which * n_z + k) * own - base
            if not 0 <= at < images:
                continue
            facts = source[pl.ds(k * block + half, FACT_ROWS), :fact_lanes][0:1].astype(jnp.float32)
            everywhere = jnp.broadcast_to(facts, (own, fact_lanes))
            label = jnp.sum(
                jnp.where(block_at, everywhere * BLOCK_ROWS, jnp.where(row_at, everywhere, 0.0)), axis=1, keepdims=True
            ).astype(jnp.int32)
            bits = jnp.zeros((own, 1), jnp.int32)
            for slot in range(slots):
                used = facts[:, slots : slots + 1] > slot
                bits = bits + jnp.where(used, 1 << facts[:, slot : slot + 1].astype(jnp.int32), 0)
            bits = jnp.where(row[:, :1] % lines < group_images, bits, 0)
            image_ref[pl.ds(at, own), 0:1] = label - cls * classes
            image_ref[pl.ds(at, own), 1:2] = bits
    embedding = jnp.dot(pooled_ref[...], whole_ref[...], preferred_element_type=jnp.float32)
    norm = jnp.sqrt(jnp.sum(embedding * embedding, axis=1, keepdims=True) + NORM_EPSILON)
    unit = embedding * (1.0 / norm)
    unit_ref[:, :embed] = unit
    unit_ref[:, embed:] = jnp.broadcast_to(norm, (images, 128))
    terms = jnp.concatenate(split(unit), axis=0)
    denom = jnp.zeros((images, 128), jnp.float32)
    picked = jnp.zeros((own, 128), jnp.float32)
    wide = 256
    for start in range(0, classes, wide):
        cols = pl.ds(start, wide)
        both = over_lanes(terms, weight_ref[cols, :])
        cosine = (both[:images] + both[images:]) * scale_ref[:, cols]
        cos_ref[:, cols] = cosine
        live, target = masks(image_ref, start, wide)
        sine = jnp.sqrt(jnp.maximum(1.0 - cosine * cosine, 0.0))
        margin = cosine * math.cos(ANGLE_MARGIN) - sine * math.sin(ANGLE_MARGIN)
        logits = LOGIT_SCALE * jnp.where(target, margin, cosine)
        exponent = jnp.where(live, jnp.exp(logits), 0.0)
        exp_ref[:, cols] = exponent
        labelled = jnp.where(target, logits, 0.0)[:own]
        chosen_ref[:, cols] = jnp.where(target[:own], scale_ref[:, cols], 0.0)
        for k in range(0, wide, 128):
            denom = denom + exponent[:, k : k + 128]
            picked = picked + labelled[:, k : k + 128]
    denom = jnp.sum(denom, axis=1, keepdims=True)
    denom_ref[...] = as_row(denom)
    weighted = split(exp_ref[:own, :] * scale_ref[...])
    chosen = split(chosen_ref[...])
    sums = jnp.dot(
        jnp.concatenate(weighted + chosen, axis=0), weight_ref[...], preferred_element_type=jnp.float32
    )
    sums = jnp.concatenate(
        [
            sums[:own] + sums[own : 2 * own],
            sums[2 * own : 3 * own] + sums[3 * own :],
            jnp.broadcast_to(denom[:own], (own, 128)),
            jnp.broadcast_to(jnp.sum(picked, axis=1, keepdims=True), (own, 128)),
        ],
        axis=1,
    )
    group_ref[...] = sums
    lines = sums_ref.shape[1]
    for step in range(n_cls):
        at = pl.multiple_of((cls ^ step) * lines, lines)
        sums_ref[step] = group_ref[pl.ds(at, lines), :]


def class_parts(own, n_cls, head_rows, slots, group_images, base, *operands):
    pooled, head, _, weight, _ = operands
    images, width = pooled.shape
    classes, embed = weight.shape
    return in_vmem(
        functools.partial(class_kernel, own, head_rows, slots, group_images, base),
        [
            f32(images, classes),
            f32(images, classes),
            f32(images, embed + 128),
            f32(n_cls, own // n_cls, 2 * embed + 256),
            f32(1, images),
            jax.ShapeDtypeStruct((images, 2), jnp.int32),
        ],
        [
            pltpu.VMEM((width, embed), jnp.bfloat16),
            pltpu.VMEM((own, classes), jnp.float32),
            pltpu.VMEM((own, 2 * embed + 256), jnp.float32),
        ],
        6,
        6 * images * embed * classes,
        operands,
    )


def grad_kernel(share, total_ref, denom_ref, exp_ref, cos_ref, unit_ref, image_ref, weight_ref, scale_ref,
                grad_ref, loss_ref, embed_ref):
    images, classes = exp_ref.shape
    embed = weight_ref.shape[1]
    at = lax.axis_index("dp") * share
    block = pl.ds(pl.multiple_of(at // 128 * 128, 128), 128)
    take = one_hot(share, 128, lambda row: row + at % 128)
    high, low = split(unit_ref[:, block])
    unit = over_lanes(take, high) + over_lanes(take, low)
    weight = over_lanes(take, weight_ref[:, block])
    denom = denom_ref[...]
    ratio = jnp.where(denom > 0.0, LOGIT_SCALE / denom, 0.0)
    left = jnp.concatenate(split(unit * ratio), axis=0)
    marked = jnp.concatenate(split(unit * LOGIT_SCALE), axis=0)
    column = jnp.broadcast_to(ratio, (128, images)).T[:, 0:1]
    dot = functools.partial(jnp.dot, preferred_element_type=jnp.float32)
    wide = 256
    for start in range(0, classes, wide):
        cols = pl.ds(start, wide)
        exponent = exp_ref[:, cols]
        _, target = masks(image_ref, start, wide)
        high, low = split(exponent)
        first = dot(left, high)
        second = dot(marked, jnp.where(target, 1.0, 0.0).astype(jnp.bfloat16))
        grad = first[:share] + first[share:] + dot(left[:share], low) - second[:share] - second[share:]
        weighted = exponent * column - jnp.where(target, LOGIT_SCALE, 0.0)
        along = jnp.sum(weighted * cos_ref[:, cols], axis=0, keepdims=True)
        scale = scale_ref[:, cols]
        grad_ref[:, cols] = (grad - weight[:, start : start + wide] * (along * scale)) * scale

    lines = padded(embed_ref.shape[0])
    own = unit_ref[pl.ds(pl.multiple_of(lax.axis_index("cls") * lines, lines), lines), :][: embed_ref.shape[0]]
    total = total_ref[: embed_ref.shape[0], :]
    weighted, picked = total[:, :embed], total[:, embed : 2 * embed]
    own_denom, target_logit = total[:, 2 * embed : 2 * embed + 1], total[:, 2 * embed + 128 : 2 * embed + 129]
    loss = jnp.broadcast_to(jnp.log(own_denom) - target_logit, (loss_ref.shape[1], 128))
    loss = jnp.concatenate([loss, jnp.zeros((128 - loss_ref.shape[1], 128), jnp.float32)], axis=0)
    loss_ref[...] = loss.T[0:1, : loss_ref.shape[1]]
    unit_grad = LOGIT_SCALE * (weighted / own_denom - picked)
    own_unit = own[:, :embed]
    embed_ref[...] = (
        unit_grad - own_unit * jnp.sum(own_unit * unit_grad, axis=1, keepdims=True)
    ) / own[:, embed : embed + 1]


def class_grad_part(share, own_images, *operands):
    images, classes = operands[2].shape
    embed = operands[6].shape[1]
    return in_vmem(
        functools.partial(grad_kernel, share),
        [f32(share, classes), f32(1, own_images), f32(own_images, embed)],
        [],
        6,
        10 * images * share * classes,
        operands,
    )


def per_device(
    attended,
    stream,
    out_proj,
    norm_gain,
    norm_shift,
    head_proj,
    class_weight,
    block_ids,
    block_count,
    labels,
):
    n_dp, n_cls = lax.axis_size("dp"), lax.axis_size("cls")
    n_z = n_dp // CORES
    dp, cls = lax.axis_index("dp"), lax.axis_index("cls")
    core = dp % CORES
    tokens, width = attended.shape
    images = tokens // P_SIZE
    size = n_cls * images
    lines = padded(images)
    group_lines = n_cls * lines
    rows = out_proj.shape[0]
    slice_rows = rows // n_cls
    slots = block_ids.shape[2]
    classes, embed = class_weight.shape

    facts = jnp.concatenate(
        [block_ids[0, 0], block_count[0], labels // BLOCK_ROWS, labels % BLOCK_ROWS]
    ).astype(jnp.bfloat16)
    n_facts = facts.shape[0]
    facts = jnp.pad(facts, (0, FACT_ROWS * embed - n_facts)).reshape(FACT_ROWS, embed)

    own_slice = lax.dynamic_slice_in_dim(out_proj, cls * slice_rows, slice_rows, 0)
    far = jnp.stack([z_swap(own_slice, step) for step in range(2, n_z)])
    near_from, _ = lax.optimization_barrier((out_proj, own_slice))
    near = z_swap(near_from, 1)
    own_other = core_swap(out_proj)
    far = after(far, own_other)
    head_rows = head_proj.shape[0]
    half = head_rows // 2
    head_half = lax.dynamic_slice_in_dim(head_proj, ((cls >> core) & 1) * half, half, 0)
    head_half = jnp.concatenate([head_half, facts], axis=0)
    from_plane = [plane_swap(far, step) for step in range(1, n_cls)]
    head_half = after(head_half, far)
    heads = [z_swap(head_half, step) for step in range(1, n_z)]
    near_other = core_swap(near)
    far = jnp.stack([far] + from_plane)
    if slice_rows % 16:
        ordered = jnp.zeros_like(far)
        for step in range(n_cls):
            ordered = lax.dynamic_update_index_in_dim(ordered, far[step], cls ^ step, 0)
        far = ordered.transpose(1, 0, 2, 3).reshape(1, n_z - 2, rows, width)
    far = after(far, near_other, *heads)
    far_other = core_swap(far)
    heads = jnp.stack(heads)
    pooled = pool_tokens(
        attended, stream, out_proj, near, own_other, near_other, far, far_other, norm_gain.reshape(1, width), norm_shift.reshape(1, width)
    )

    column = jnp.stack([pooled] + [z_swap(pooled, step) for step in range(1, n_z)])
    heads = jnp.concatenate([head_half[None], heads], axis=0)
    counterparts = half_swap(heads)

    scale = lax.rsqrt(
        jnp.sum(jnp.square(class_weight.astype(jnp.float32)), axis=1) + NORM_EPSILON
    )[None, :]

    groups = jnp.zeros((n_z, n_cls, lines, width), pooled.dtype)
    from_plane = [plane_swap(column, step) for step in range(1, n_cls)]
    for step, got in enumerate([column] + from_plane):
        groups = lax.dynamic_update_slice_in_dim(groups, got[:, None], cls ^ step, 1)
    counterparts = after(counterparts, from_plane[0])
    heads = jnp.concatenate([heads.reshape(-1, embed), counterparts.reshape(-1, embed)], axis=0)
    other_heads = core_swap(heads)
    groups = jnp.concatenate([groups, core_swap(groups)], axis=0)
    pooled_all = groups.reshape(n_dp * group_lines, width)

    piece = group_lines * max(1, min(n_dp, 256 // group_lines))
    total_lines = n_dp * group_lines
    parts = [
        class_parts(
            group_lines, n_cls, head_rows, slots, images, at, pooled_all[at : at + piece], heads, other_heads, class_weight, scale
        )
        for at in range(0, total_lines, piece)
    ]
    denoms = jnp.concatenate([p[4] for p in parts], axis=1)
    sums = parts[0][3]
    extra = -(-total_lines // sums.shape[2])
    denoms = jnp.pad(denoms, ((0, 0), (0, extra * sums.shape[2] - total_lines))).reshape(extra, -1)

    def packed(step):
        return jnp.concatenate([sums[step, :images], denoms], axis=0)

    total = packed(0)
    for step in range(n_cls - 1, 0, -1):
        total = total + plane_swap(packed(step), step)
    denominator = total[images:].reshape(1, -1)[:, :total_lines]
    share = embed // n_dp
    for k, (exponent, cosine, unit, _, _, image_facts) in enumerate(parts):
        at = k * piece
        grad, loss, embed_part = class_grad_part(
            share, images, total, denominator[:, at : at + piece], exponent, cosine, unit,
            image_facts, class_weight, scale,
        )
        if k == 0:
            class_grad, sample_loss, embed_grad = grad, loss, embed_part
        else:
            class_grad = class_grad + grad
    return (sample_loss.reshape(images), embed_grad, class_grad.T)


def solution(mesh):
    placed = (
        P(("dp", "cls"), None),
        P(("dp", "cls"), None),
        P("dp", None),
        P(),
        P(),
        P("dp", None),
        P("cls", None),
        P("dp", "cls", None),
        P("dp", "cls"),
        P("dp"),
    )
    return jax.shard_map(
        per_device,
        mesh=mesh,
        in_specs=placed,
        out_specs=(P(("dp", "cls")), P(("dp", "cls"), None), P("cls", "dp")),
        check_vma=False,
    )
```

```python
import functools
import math

import jax
import jax.numpy as jnp
from jax import lax
from jax.experimental import pallas as pl
from jax.experimental.pallas import tpu as pltpu
from jax.sharding import PartitionSpec as P

P_SIZE = 144
BLOCK_ROWS = 128
CORES = 2
FACT_ROWS = 16

LOGIT_SCALE = 64.0
ANGLE_MARGIN = 0.5
NORM_EPSILON = 1e-06


def z_swap(value, step):
    count = lax.axis_size("dp")
    return lax.ppermute(value, "dp", [(i, i ^ (step * CORES)) for i in range(count)])


def core_swap(value):
    count = lax.axis_size("dp")
    return lax.ppermute(value, "dp", [(i, i ^ 1) for i in range(count)])


def half_swap(value):
    n_dp, n_cls = lax.axis_size("dp"), lax.axis_size("cls")
    pairs = [(dp * n_cls + c, dp * n_cls + (c ^ (1 << dp % CORES))) for dp in range(n_dp) for c in range(n_cls)]
    return lax.ppermute(value, ("dp", "cls"), pairs)


def plane_swap(value, step):
    count = lax.axis_size("cls")
    return lax.ppermute(value, "cls", [(i, i ^ step) for i in range(count)])


def pool_kernel(att_ref, stream_ref, own_ref, near_ref, own_other_ref, near_other_ref, far_ref, far_other_ref, gain_ref, shift_ref,
                out_ref, weight_ref, mixed_ref, pooled_ref):
    tokens, width = stream_ref.shape
    images = tokens // P_SIZE
    chunk = mixed_ref.shape[0]
    pieces = range(0, tokens, chunk)
    n_cls, n_far, slice_rows, _ = far_ref.shape
    rows = n_cls * slice_rows
    dp, cls = lax.axis_index("dp"), lax.axis_index("cls")
    z, core = dp // CORES, dp % CORES

    def place(shard, start, value):
        at = pl.multiple_of(shard * rows + start, slice_rows)
        weight_ref[pl.ds(at, value.shape[0]), :] = value

    for side, own, near, far in (
        (core, own_ref, near_ref, far_ref), (1 - core, own_other_ref, near_other_ref, far_other_ref)
    ):
        place(z * CORES + side, 0, own[...])
        place((z ^ 1) * CORES + side, 0, near[...])
        for k in range(n_far):
            for step in range(n_cls):
                start = (cls ^ step) * slice_rows if n_cls > 1 else 0
                place((z ^ (k + 2)) * CORES + side, start, far[step, k])
    step = 24
    for k, start in enumerate(pieces):
        mixed_ref[...] = jnp.dot(
            att_ref[pl.ds(start, chunk), :], weight_ref[...], preferred_element_type=jnp.float32
        )
        for image in range(chunk // P_SIZE):
            total = jnp.zeros((8, width), jnp.float32)
            for r in range(0, P_SIZE, step):
                at = image * P_SIZE + r
                x = mixed_ref[pl.ds(at, step), :] + stream_ref[pl.ds(start + at, step), :].astype(jnp.float32)
                centred = x - jnp.mean(x, axis=1, keepdims=True)
                variance = jnp.mean(centred * centred, axis=1, keepdims=True)
                scaled = centred * lax.rsqrt(variance + NORM_EPSILON)
                total = total + jnp.sum(scaled.reshape(step // 8, 8, width), axis=0)
            mean = jnp.sum(total, axis=0, keepdims=True) * (1.0 / P_SIZE)
            pooled_ref[pl.ds(start // P_SIZE + image, 1), :] = gain_ref[...] * mean + shift_ref[...]
    if images < pooled_ref.shape[0]:
        pooled_ref[images:, :] = jnp.zeros((pooled_ref.shape[0] - images, width), jnp.float32)
    out_ref[...] = pooled_ref[...].astype(out_ref.dtype)


def padded(images):
    return -(-images // 8) * 8


def after(value, *others):
    anywhere = pl.BlockSpec(memory_space=pl.ANY)
    return pl.pallas_call(
        lambda *refs: None,
        out_shape=jax.ShapeDtypeStruct(value.shape, value.dtype),
        in_specs=[anywhere] * (1 + len(others)),
        out_specs=anywhere,
        input_output_aliases={0: 0},
        compiler_params=pltpu.CompilerParams(vmem_limit_bytes=1024 * 1024),
    )(value, *others)


def in_vmem(kernel, outs, scratch, mib, flops, operands, in_hbm=0):
    vmem = pl.BlockSpec(memory_space=pltpu.VMEM)
    moved = sum(math.prod(x.shape) * x.dtype.itemsize for x in list(operands) + list(outs))
    return pl.pallas_call(
        kernel,
        out_shape=tuple(outs),
        in_specs=[pl.BlockSpec(memory_space=pl.ANY)] * in_hbm + [vmem] * (len(operands) - in_hbm),
        out_specs=(vmem,) * len(outs),
        scratch_shapes=scratch,
        compiler_params=pltpu.CompilerParams(vmem_limit_bytes=mib * 1024 * 1024),
        cost_estimate=pl.CostEstimate(flops=flops, bytes_accessed=moved, transcendentals=0),
    )(*operands)


def f32(*shape):
    return jax.ShapeDtypeStruct(shape, jnp.float32)


def pool_tokens(*operands):
    tokens, width = operands[0].shape
    images = tokens // P_SIZE
    lines = padded(images)
    chunk = (3 if images % 3 == 0 else 1) * P_SIZE
    return in_vmem(
        pool_kernel,
        [jax.ShapeDtypeStruct((lines, width), jnp.bfloat16)],
        [
            pltpu.VMEM((width, width), jnp.bfloat16),
            pltpu.VMEM((chunk, width), jnp.float32),
            pltpu.VMEM((lines, width), jnp.float32),
        ],
        12,
        2 * tokens * width * width,
        operands,
    )[0]


def split(value):
    high = value.astype(jnp.bfloat16)
    return high, (value - high.astype(jnp.float32)).astype(jnp.bfloat16)


def as_row(column):
    return jnp.broadcast_to(column, (column.shape[0], 128)).T[0:1]


def over_lanes(left, right):
    return lax.dot_general(left, right, (((1,), (1,)), ((), ())), preferred_element_type=jnp.float32)


def one_hot(rows, columns, at):
    row = lax.broadcasted_iota(jnp.int32, (rows, columns), 0)
    column = lax.broadcasted_iota(jnp.int32, (rows, columns), 1)
    return jnp.where(column == at(row), 1.0, 0.0).astype(jnp.bfloat16)


def masks(image_ref, start, wide):
    images = image_ref.shape[0]
    label, bits = image_ref[:, 0:1], image_ref[:, 1:2]
    live = [
        jnp.broadcast_to((bits & (1 << (k // BLOCK_ROWS))) != 0, (images, BLOCK_ROWS))
        for k in range(start, start + wide, BLOCK_ROWS)
    ]
    live = jnp.concatenate(live, axis=1)
    column = lax.broadcasted_iota(jnp.int32, (images, wide), 1) + start
    return live, live & (column == label)


def facts_kernel(own, slots, group_images, n_cls, classes, head_ref, other_ref, whole_ref, image_ref):
    width = whole_ref.shape[0]
    n_z = image_ref.shape[0] // (CORES * own)
    dp, cls = lax.axis_index("dp"), lax.axis_index("cls")
    z, core = dp // CORES, dp % CORES
    head_rows = width // (CORES * n_z)
    half = head_rows // 2
    block = half + FACT_ROWS
    size = group_images * n_cls
    lines = own // n_cls
    fact_lanes = -(-(slots + 1 + 2 * size) // 128) * 128
    row = lax.broadcasted_iota(jnp.int32, (own, fact_lanes), 0)
    lane = lax.broadcasted_iota(jnp.int32, (own, fact_lanes), 1)
    image = slots + 1 + row // lines * group_images + row % lines
    block_at = (lane == image) & (row % lines < group_images)
    row_at = (lane == image + size) & (row % lines < group_images)
    for side, source in ((core, head_ref), (1 - core, other_ref)):
        mine = (cls >> side) & 1
        for k in range(n_z):
            for part, which in ((0, mine), (1, 1 - mine)):
                at = pl.multiple_of(((z ^ k) * CORES + side) * head_rows + which * half, half)
                whole_ref[pl.ds(at, half), :] = source[pl.ds((part * n_z + k) * block, half), :]
    for which, source in enumerate((head_ref, other_ref)):
        for k in range(n_z):
            at = (which * n_z + k) * own
            facts = source[pl.ds(k * block + half, FACT_ROWS), :fact_lanes][0:1].astype(jnp.float32)
            everywhere = jnp.broadcast_to(facts, (own, fact_lanes))
            label = jnp.sum(
                jnp.where(block_at, everywhere * BLOCK_ROWS, jnp.where(row_at, everywhere, 0.0)), axis=1, keepdims=True
            ).astype(jnp.int32)
            bits = jnp.zeros((own, 1), jnp.int32)
            for slot in range(slots):
                used = facts[:, slots : slots + 1] > slot
                bits = bits + jnp.where(used, 1 << facts[:, slot : slot + 1].astype(jnp.int32), 0)
            bits = jnp.where(row[:, :1] % lines < group_images, bits, 0)
            image_ref[pl.ds(at, own), 0:1] = label - cls * classes
            image_ref[pl.ds(at, own), 1:2] = bits


def group_facts(own, slots, group_images, n_cls, classes, width, total, *operands):
    embed = operands[0].shape[1]
    return in_vmem(
        functools.partial(facts_kernel, own, slots, group_images, n_cls, classes),
        [jax.ShapeDtypeStruct((width, embed), jnp.bfloat16), jax.ShapeDtypeStruct((total, 2), jnp.int32)],
        [],
        4,
        0,
        operands,
    )


def class_kernel(own, pooled_ref, whole_ref, image_ref, weight_ref, scale_ref,
                 exp_ref, cos_ref, unit_ref, sums_ref, denom_ref, chosen_ref, group_ref):
    images = pooled_ref.shape[0]
    classes, embed = weight_ref.shape
    n_cls = sums_ref.shape[0]
    cls = lax.axis_index("cls")
    embedding = jnp.dot(pooled_ref[...], whole_ref[...], preferred_element_type=jnp.float32)
    norm = jnp.sqrt(jnp.sum(embedding * embedding, axis=1, keepdims=True) + NORM_EPSILON)
    unit = embedding * (1.0 / norm)
    unit_ref[:, :embed] = unit
    unit_ref[:, embed:] = jnp.broadcast_to(norm, (images, 128))
    terms = jnp.concatenate(split(unit), axis=0)
    denom = jnp.zeros((images, 128), jnp.float32)
    picked = jnp.zeros((own, 128), jnp.float32)
    wide = 256
    for start in range(0, classes, wide):
        cols = pl.ds(start, wide)
        both = over_lanes(terms, weight_ref[cols, :])
        cosine = (both[:images] + both[images:]) * scale_ref[:, cols]
        cos_ref[:, cols] = cosine
        live, target = masks(image_ref, start, wide)
        sine = jnp.sqrt(jnp.maximum(1.0 - cosine * cosine, 0.0))
        margin = cosine * math.cos(ANGLE_MARGIN) - sine * math.sin(ANGLE_MARGIN)
        logits = LOGIT_SCALE * jnp.where(target, margin, cosine)
        exponent = jnp.where(live, jnp.exp(logits), 0.0)
        exp_ref[:, cols] = exponent
        labelled = jnp.where(target, logits, 0.0)[:own]
        chosen_ref[:, cols] = jnp.where(target[:own], scale_ref[:, cols], 0.0)
        for k in range(0, wide, 128):
            denom = denom + exponent[:, k : k + 128]
            picked = picked + labelled[:, k : k + 128]
    denom = jnp.sum(denom, axis=1, keepdims=True)
    denom_ref[...] = as_row(denom)
    weighted = split(exp_ref[:own, :] * scale_ref[...])
    chosen = split(chosen_ref[...])
    sums = jnp.dot(
        jnp.concatenate(weighted + chosen, axis=0), weight_ref[...], preferred_element_type=jnp.float32
    )
    sums = jnp.concatenate(
        [
            sums[:own] + sums[own : 2 * own],
            sums[2 * own : 3 * own] + sums[3 * own :],
            jnp.broadcast_to(denom[:own], (own, 128)),
            jnp.broadcast_to(jnp.sum(picked, axis=1, keepdims=True), (own, 128)),
        ],
        axis=1,
    )
    group_ref[...] = sums
    lines = sums_ref.shape[1]
    for step in range(n_cls):
        at = pl.multiple_of((cls ^ step) * lines, lines)
        sums_ref[step] = group_ref[pl.ds(at, lines), :]


def class_parts(own, n_cls, *operands):
    pooled, _, _, weight, _ = operands
    images, width = pooled.shape
    classes, embed = weight.shape
    return in_vmem(
        functools.partial(class_kernel, own),
        [
            f32(images, classes),
            f32(images, classes),
            f32(images, embed + 128),
            f32(n_cls, own // n_cls, 2 * embed + 256),
            f32(1, images),
        ],
        [
            pltpu.VMEM((own, classes), jnp.float32),
            pltpu.VMEM((own, 2 * embed + 256), jnp.float32),
        ],
        6,
        6 * images * embed * classes,
        operands,
    )


def aside_kernel(share, exp_ref, cos_ref, unit_ref, image_ref, weight_ref,
                 high_ref, low_ref, along_ref, unit_out, weight_out, marked_ref, mark_ref):
    images, classes = exp_ref.shape
    at = lax.axis_index("dp") * share
    block = pl.ds(pl.multiple_of(at // 128 * 128, 128), 128)
    take = one_hot(share, 128, lambda row: row + at % 128)
    high, low = split(unit_ref[:, block])
    unit = over_lanes(take, high) + over_lanes(take, low)
    unit_out[...] = unit
    weight_out[...] = over_lanes(take, weight_ref[:, block])
    marked = jnp.concatenate(split(unit * LOGIT_SCALE), axis=0)
    wide = 256
    for start in range(0, classes, wide):
        cols = pl.ds(start, wide)
        exponent, cosine = exp_ref[:, cols], cos_ref[:, cols]
        _, target = masks(image_ref, start, wide)
        high_ref[:, cols], low_ref[:, cols] = split(exponent)
        along_ref[:, cols] = exponent * cosine
        mark_ref[:, cols] = jnp.sum(jnp.where(target, LOGIT_SCALE * cosine, 0.0), axis=0, keepdims=True)
        both = jnp.dot(
            marked, jnp.where(target, 1.0, 0.0).astype(jnp.bfloat16), preferred_element_type=jnp.float32
        )
        marked_ref[:, cols] = both[:share] + both[share:]


def class_grad_aside(share, *operands):
    images, classes = operands[0].shape
    return in_vmem(
        functools.partial(aside_kernel, share),
        [
            jax.ShapeDtypeStruct((images, classes), jnp.bfloat16),
            jax.ShapeDtypeStruct((images, classes), jnp.bfloat16),
            f32(images, classes),
            f32(share, images),
            f32(share, classes),
            f32(share, classes),
            f32(1, classes),
        ],
        [],
        5,
        4 * images * share * classes,
        operands,
    )


def grad_kernel(total_ref, denom_ref, high_ref, low_ref, along_ref, unit_share_ref, weight_share_ref, marked_ref,
                mark_ref, scale_ref, unit_ref, grad_ref, loss_ref, embed_ref):
    images, classes = high_ref.shape
    share = unit_share_ref.shape[0]
    embed = embed_ref.shape[1]
    denom = denom_ref[...]
    ratio = jnp.where(denom > 0.0, LOGIT_SCALE / denom, 0.0)
    left = jnp.concatenate(split(unit_share_ref[...] * ratio), axis=0)
    column = jnp.broadcast_to(ratio, (128, images)).T[:, 0:1]
    dot = functools.partial(jnp.dot, preferred_element_type=jnp.float32)
    wide = 256
    for start in range(0, classes, wide):
        cols = pl.ds(start, wide)
        first = dot(left, high_ref[:, cols])
        grad = first[:share] + first[share:] + dot(left[:share], low_ref[:, cols]) - marked_ref[:, cols]
        along = jnp.sum(along_ref[:, cols] * column, axis=0, keepdims=True) - mark_ref[:, cols]
        scale = scale_ref[:, cols]
        grad_ref[:, cols] = (grad - weight_share_ref[:, cols] * (along * scale)) * scale

    lines = padded(embed_ref.shape[0])
    own = unit_ref[pl.ds(pl.multiple_of(lax.axis_index("cls") * lines, lines), lines), :][: embed_ref.shape[0]]
    total = total_ref[: embed_ref.shape[0], :]
    weighted, picked = total[:, :embed], total[:, embed : 2 * embed]
    own_denom, target_logit = total[:, 2 * embed : 2 * embed + 1], total[:, 2 * embed + 128 : 2 * embed + 129]
    loss = jnp.broadcast_to(jnp.log(own_denom) - target_logit, (loss_ref.shape[1], 128))
    loss = jnp.concatenate([loss, jnp.zeros((128 - loss_ref.shape[1], 128), jnp.float32)], axis=0)
    loss_ref[...] = loss.T[0:1, : loss_ref.shape[1]]
    unit_grad = LOGIT_SCALE * (weighted / own_denom - picked)
    own_unit = own[:, :embed]
    embed_ref[...] = (
        unit_grad - own_unit * jnp.sum(own_unit * unit_grad, axis=1, keepdims=True)
    ) / own[:, embed : embed + 1]


def class_grad_part(own_images, *operands):
    images, classes = operands[2].shape
    share = operands[5].shape[0]
    embed = operands[10].shape[1] - 128
    return in_vmem(
        grad_kernel,
        [f32(share, classes), f32(1, own_images), f32(own_images, embed)],
        [],
        5,
        6 * images * share * classes,
        operands,
    )


def per_device(
    attended,
    stream,
    out_proj,
    norm_gain,
    norm_shift,
    head_proj,
    class_weight,
    block_ids,
    block_count,
    labels,
):
    n_dp, n_cls = lax.axis_size("dp"), lax.axis_size("cls")
    n_z = n_dp // CORES
    dp, cls = lax.axis_index("dp"), lax.axis_index("cls")
    core = dp % CORES
    tokens, width = attended.shape
    images = tokens // P_SIZE
    size = n_cls * images
    lines = padded(images)
    group_lines = n_cls * lines
    rows = out_proj.shape[0]
    slice_rows = rows // n_cls
    slots = block_ids.shape[2]
    classes, embed = class_weight.shape

    facts = jnp.concatenate(
        [block_ids[0, 0], block_count[0], labels // BLOCK_ROWS, labels % BLOCK_ROWS]
    ).astype(jnp.bfloat16)
    n_facts = facts.shape[0]
    facts = jnp.pad(facts, (0, FACT_ROWS * embed - n_facts)).reshape(FACT_ROWS, embed)

    own_slice = lax.dynamic_slice_in_dim(out_proj, cls * slice_rows, slice_rows, 0)
    far = jnp.stack([z_swap(own_slice, step) for step in range(2, n_z)])
    near_from, _ = lax.optimization_barrier((out_proj, own_slice))
    near = z_swap(near_from, 1)
    own_other = core_swap(out_proj)
    far = after(far, own_other)
    head_rows = head_proj.shape[0]
    half = head_rows // 2
    head_half = lax.dynamic_slice_in_dim(head_proj, ((cls >> core) & 1) * half, half, 0)
    head_half = jnp.concatenate([head_half, facts], axis=0)
    from_plane = [plane_swap(far, step) for step in range(1, n_cls)]
    head_half = after(head_half, far)
    heads = [z_swap(head_half, step) for step in range(1, n_z)]
    near_other = core_swap(near)
    far = jnp.stack([far] + from_plane)
    if slice_rows % 16:
        ordered = jnp.zeros_like(far)
        for step in range(n_cls):
            ordered = lax.dynamic_update_index_in_dim(ordered, far[step], cls ^ step, 0)
        far = ordered.transpose(1, 0, 2, 3).reshape(1, n_z - 2, rows, width)
    far = after(far, near_other, *heads)
    far_other = core_swap(far)
    heads = jnp.stack(heads)
    pooled = pool_tokens(
        attended, stream, out_proj, near, own_other, near_other, far, far_other, norm_gain.reshape(1, width), norm_shift.reshape(1, width)
    )

    column = jnp.stack([pooled] + [z_swap(pooled, step) for step in range(1, n_z)])
    heads = jnp.concatenate([head_half[None], heads], axis=0)
    counterparts = half_swap(heads)

    scale = lax.rsqrt(
        jnp.sum(jnp.square(class_weight.astype(jnp.float32)), axis=1) + NORM_EPSILON
    )[None, :]

    groups = jnp.zeros((n_z, n_cls, lines, width), pooled.dtype)
    from_plane = [plane_swap(column, step) for step in range(1, n_cls)]
    for step, got in enumerate([column] + from_plane):
        groups = lax.dynamic_update_slice_in_dim(groups, got[:, None], cls ^ step, 1)
    counterparts = after(counterparts, from_plane[0])
    heads = jnp.concatenate([heads.reshape(-1, embed), counterparts.reshape(-1, embed)], axis=0)
    other_heads = core_swap(heads)
    total_lines = n_dp * group_lines
    whole_head, image_facts = group_facts(
        group_lines, slots, images, n_cls, classes, width, total_lines, heads, other_heads
    )
    groups = jnp.concatenate([groups, after(core_swap(groups), whole_head)], axis=0)
    pooled_all = groups.reshape(n_dp * group_lines, width)

    piece = group_lines * max(1, min(n_dp, 256 // group_lines))
    pieces = [slice(at, at + piece) for at in range(0, total_lines, piece)]
    parts = [
        class_parts(group_lines, n_cls, pooled_all[at], whole_head, image_facts[at], class_weight, scale)
        for at in pieces
    ]
    denoms = jnp.concatenate([p[4] for p in parts], axis=1)
    sums = parts[0][3]
    extra = -(-total_lines // sums.shape[2])
    denoms = jnp.pad(denoms, ((0, 0), (0, extra * sums.shape[2] - total_lines))).reshape(extra, -1)

    def packed(step):
        return jnp.concatenate([sums[step, :images], denoms], axis=0)

    total = packed(0)
    for step in range(n_cls - 1, 0, -1):
        total = total + plane_swap(packed(step), step)
    denominator = total[images:].reshape(1, -1)[:, :total_lines]
    share = embed // n_dp
    for k, (at, (exponent, cosine, unit, _, _)) in enumerate(zip(pieces, parts)):
        aside = class_grad_aside(share, exponent, cosine, unit, image_facts[at], class_weight)
        grad, loss, embed_part = class_grad_part(images, total, denominator[:, at], *aside, scale, unit)
        if k == 0:
            class_grad, sample_loss, embed_grad = grad, loss, embed_part
        else:
            class_grad = class_grad + grad
    return (sample_loss.reshape(images), embed_grad, class_grad.T)


def solution(mesh):
    placed = (
        P(("dp", "cls"), None),
        P(("dp", "cls"), None),
        P("dp", None),
        P(),
        P(),
        P("dp", None),
        P("cls", None),
        P("dp", "cls", None),
        P("dp", "cls"),
        P("dp"),
    )
    return jax.shard_map(
        per_device,
        mesh=mesh,
        in_specs=placed,
        out_specs=(P(("dp", "cls")), P(("dp", "cls"), None), P("cls", "dp")),
        check_vma=False,
    )
```

```python
import functools
import math

import jax
import jax.numpy as jnp
from jax import lax
from jax.experimental import pallas as pl
from jax.experimental.pallas import tpu as pltpu
from jax.sharding import PartitionSpec as P

P_SIZE = 144
BLOCK_ROWS = 128
CORES = 2
FACT_ROWS = 16

LOGIT_SCALE = 64.0
ANGLE_MARGIN = 0.5
NORM_EPSILON = 1e-06


def z_swap(value, step):
    count = lax.axis_size("dp")
    return lax.ppermute(value, "dp", [(i, i ^ (step * CORES)) for i in range(count)])


def core_swap(value):
    count = lax.axis_size("dp")
    return lax.ppermute(value, "dp", [(i, i ^ 1) for i in range(count)])


def half_swap(value):
    n_dp, n_cls = lax.axis_size("dp"), lax.axis_size("cls")
    pairs = [(dp * n_cls + c, dp * n_cls + (c ^ (1 << dp % CORES))) for dp in range(n_dp) for c in range(n_cls)]
    return lax.ppermute(value, ("dp", "cls"), pairs)


def plane_swap(value, step):
    count = lax.axis_size("cls")
    return lax.ppermute(value, "cls", [(i, i ^ step) for i in range(count)])


def pool_kernel(att_ref, stream_ref, own_ref, near_ref, own_other_ref, near_other_ref, far_ref, far_other_ref, gain_ref, shift_ref,
                out_ref, weight_ref, mixed_ref, pooled_ref):
    tokens, width = stream_ref.shape
    images = tokens // P_SIZE
    chunk = mixed_ref.shape[0]
    pieces = range(0, tokens, chunk)
    n_cls, n_far, slice_rows, _ = far_ref.shape
    rows = n_cls * slice_rows
    dp, cls = lax.axis_index("dp"), lax.axis_index("cls")
    z, core = dp // CORES, dp % CORES

    def place(shard, start, value):
        at = pl.multiple_of(shard * rows + start, slice_rows)
        weight_ref[pl.ds(at, value.shape[0]), :] = value

    for side, own, near, far in (
        (core, own_ref, near_ref, far_ref), (1 - core, own_other_ref, near_other_ref, far_other_ref)
    ):
        place(z * CORES + side, 0, own[...])
        place((z ^ 1) * CORES + side, 0, near[...])
        for k in range(n_far):
            for step in range(n_cls):
                start = (cls ^ step) * slice_rows if n_cls > 1 else 0
                place((z ^ (k + 2)) * CORES + side, start, far[step, k])
    step = 24
    for k, start in enumerate(pieces):
        mixed_ref[...] = jnp.dot(
            att_ref[pl.ds(start, chunk), :], weight_ref[...], preferred_element_type=jnp.float32
        )
        for image in range(chunk // P_SIZE):
            total = jnp.zeros((8, width), jnp.float32)
            for r in range(0, P_SIZE, step):
                at = image * P_SIZE + r
                x = mixed_ref[pl.ds(at, step), :] + stream_ref[pl.ds(start + at, step), :].astype(jnp.float32)
                centred = x - jnp.mean(x, axis=1, keepdims=True)
                variance = jnp.mean(centred * centred, axis=1, keepdims=True)
                scaled = centred * lax.rsqrt(variance + NORM_EPSILON)
                total = total + jnp.sum(scaled.reshape(step // 8, 8, width), axis=0)
            mean = jnp.sum(total, axis=0, keepdims=True) * (1.0 / P_SIZE)
            pooled_ref[pl.ds(start // P_SIZE + image, 1), :] = gain_ref[...] * mean + shift_ref[...]
    if images < pooled_ref.shape[0]:
        pooled_ref[images:, :] = jnp.zeros((pooled_ref.shape[0] - images, width), jnp.float32)
    out_ref[...] = pooled_ref[...].astype(out_ref.dtype)


def padded(images):
    return -(-images // 8) * 8


def after(value, *others):
    anywhere = pl.BlockSpec(memory_space=pl.ANY)
    return pl.pallas_call(
        lambda *refs: None,
        out_shape=jax.ShapeDtypeStruct(value.shape, value.dtype),
        in_specs=[anywhere] * (1 + len(others)),
        out_specs=anywhere,
        input_output_aliases={0: 0},
        compiler_params=pltpu.CompilerParams(vmem_limit_bytes=1024 * 1024),
    )(value, *others)


def in_vmem(kernel, outs, scratch, mib, flops, operands, in_hbm=0):
    vmem = pl.BlockSpec(memory_space=pltpu.VMEM)
    moved = sum(math.prod(x.shape) * x.dtype.itemsize for x in list(operands) + list(outs))
    return pl.pallas_call(
        kernel,
        out_shape=tuple(outs),
        in_specs=[pl.BlockSpec(memory_space=pl.ANY)] * in_hbm + [vmem] * (len(operands) - in_hbm),
        out_specs=(vmem,) * len(outs),
        scratch_shapes=scratch,
        compiler_params=pltpu.CompilerParams(vmem_limit_bytes=mib * 1024 * 1024),
        cost_estimate=pl.CostEstimate(flops=flops, bytes_accessed=moved, transcendentals=0),
    )(*operands)


def f32(*shape):
    return jax.ShapeDtypeStruct(shape, jnp.float32)


def pool_tokens(*operands):
    tokens, width = operands[0].shape
    images = tokens // P_SIZE
    lines = padded(images)
    chunk = (3 if images % 3 == 0 else 1) * P_SIZE
    return in_vmem(
        pool_kernel,
        [jax.ShapeDtypeStruct((lines, width), jnp.bfloat16)],
        [
            pltpu.VMEM((width, width), jnp.bfloat16),
            pltpu.VMEM((chunk, width), jnp.float32),
            pltpu.VMEM((lines, width), jnp.float32),
        ],
        12,
        2 * tokens * width * width,
        operands,
    )[0]


def split(value):
    high = value.astype(jnp.bfloat16)
    return high, (value - high.astype(jnp.float32)).astype(jnp.bfloat16)


def as_row(column):
    return jnp.broadcast_to(column, (column.shape[0], 128)).T[0:1]


def over_lanes(left, right):
    return lax.dot_general(left, right, (((1,), (1,)), ((), ())), preferred_element_type=jnp.float32)


def one_hot(rows, columns, at):
    row = lax.broadcasted_iota(jnp.int32, (rows, columns), 0)
    column = lax.broadcasted_iota(jnp.int32, (rows, columns), 1)
    return jnp.where(column == at(row), 1.0, 0.0).astype(jnp.bfloat16)


def masks(image_ref, start, wide):
    images = image_ref.shape[0]
    label, bits = image_ref[:, 0:1], image_ref[:, 1:2]
    live = [
        jnp.broadcast_to((bits & (1 << (k // BLOCK_ROWS))) != 0, (images, BLOCK_ROWS))
        for k in range(start, start + wide, BLOCK_ROWS)
    ]
    live = jnp.concatenate(live, axis=1)
    column = lax.broadcasted_iota(jnp.int32, (images, wide), 1) + start
    return live, live & (column == label)


def facts_kernel(own, slots, group_images, n_cls, classes, head_ref, other_ref, whole_ref, image_ref):
    width = whole_ref.shape[0]
    n_z = image_ref.shape[0] // (CORES * own)
    dp, cls = lax.axis_index("dp"), lax.axis_index("cls")
    z, core = dp // CORES, dp % CORES
    head_rows = width // (CORES * n_z)
    half = head_rows // 2
    block = half + FACT_ROWS
    size = group_images * n_cls
    lines = own // n_cls
    fact_lanes = -(-(slots + 1 + 2 * size) // 128) * 128
    row = lax.broadcasted_iota(jnp.int32, (own, fact_lanes), 0)
    lane = lax.broadcasted_iota(jnp.int32, (own, fact_lanes), 1)
    image = slots + 1 + row // lines * group_images + row % lines
    block_at = (lane == image) & (row % lines < group_images)
    row_at = (lane == image + size) & (row % lines < group_images)
    for side, source in ((core, head_ref), (1 - core, other_ref)):
        mine = (cls >> side) & 1
        for k in range(n_z):
            for part, which in ((0, mine), (1, 1 - mine)):
                at = pl.multiple_of(((z ^ k) * CORES + side) * head_rows + which * half, half)
                whole_ref[pl.ds(at, half), :] = source[pl.ds((part * n_z + k) * block, half), :]
    for which, source in enumerate((head_ref, other_ref)):
        for k in range(n_z):
            at = (which * n_z + k) * own
            facts = source[pl.ds(k * block + half, FACT_ROWS), :fact_lanes][0:1].astype(jnp.float32)
            everywhere = jnp.broadcast_to(facts, (own, fact_lanes))
            label = jnp.sum(
                jnp.where(block_at, everywhere * BLOCK_ROWS, jnp.where(row_at, everywhere, 0.0)), axis=1, keepdims=True
            ).astype(jnp.int32)
            bits = jnp.zeros((own, 1), jnp.int32)
            for slot in range(slots):
                used = facts[:, slots : slots + 1] > slot
                bits = bits + jnp.where(used, 1 << facts[:, slot : slot + 1].astype(jnp.int32), 0)
            bits = jnp.where(row[:, :1] % lines < group_images, bits, 0)
            image_ref[pl.ds(at, own), 0:1] = label - cls * classes
            image_ref[pl.ds(at, own), 1:2] = bits


def group_facts(own, slots, group_images, n_cls, classes, width, total, *operands):
    embed = operands[0].shape[1]
    return in_vmem(
        functools.partial(facts_kernel, own, slots, group_images, n_cls, classes),
        [jax.ShapeDtypeStruct((width, embed), jnp.bfloat16), jax.ShapeDtypeStruct((total, 2), jnp.int32)],
        [],
        4,
        0,
        operands,
    )


def class_kernel(own, pooled_ref, whole_ref, image_ref, weight_ref, scale_ref,
                 exp_ref, cos_ref, unit_ref, sums_ref, denom_ref, chosen_ref, group_ref):
    images = pooled_ref.shape[0]
    classes, embed = weight_ref.shape
    n_cls = sums_ref.shape[0]
    cls = lax.axis_index("cls")
    embedding = jnp.dot(pooled_ref[...], whole_ref[...], preferred_element_type=jnp.float32)
    norm = jnp.sqrt(jnp.sum(embedding * embedding, axis=1, keepdims=True) + NORM_EPSILON)
    unit = embedding * (1.0 / norm)
    unit_ref[:, :embed] = unit
    unit_ref[:, embed:] = jnp.broadcast_to(norm, (images, 128))
    terms = jnp.concatenate(split(unit), axis=0)
    denom = jnp.zeros((images, 128), jnp.float32)
    picked = jnp.zeros((own, 128), jnp.float32)
    wide = 256
    for start in range(0, classes, wide):
        cols = pl.ds(start, wide)
        both = over_lanes(terms, weight_ref[cols, :])
        cosine = (both[:images] + both[images:]) * scale_ref[:, cols]
        cos_ref[:, cols] = cosine
        live, target = masks(image_ref, start, wide)
        sine = jnp.sqrt(jnp.maximum(1.0 - cosine * cosine, 0.0))
        margin = cosine * math.cos(ANGLE_MARGIN) - sine * math.sin(ANGLE_MARGIN)
        logits = LOGIT_SCALE * jnp.where(target, margin, cosine)
        exponent = jnp.where(live, jnp.exp(logits), 0.0)
        exp_ref[:, cols] = exponent
        labelled = jnp.where(target, logits, 0.0)[:own]
        chosen_ref[:, cols] = jnp.where(target[:own], scale_ref[:, cols], 0.0)
        for k in range(0, wide, 128):
            denom = denom + exponent[:, k : k + 128]
            picked = picked + labelled[:, k : k + 128]
    denom = jnp.sum(denom, axis=1, keepdims=True)
    denom_ref[...] = as_row(denom)
    weighted = split(exp_ref[:own, :] * scale_ref[...])
    chosen = split(chosen_ref[...])
    sums = jnp.dot(
        jnp.concatenate(weighted + chosen, axis=0), weight_ref[...], preferred_element_type=jnp.float32
    )
    sums = jnp.concatenate(
        [
            sums[:own] + sums[own : 2 * own],
            sums[2 * own : 3 * own] + sums[3 * own :],
            jnp.broadcast_to(denom[:own], (own, 128)),
            jnp.broadcast_to(jnp.sum(picked, axis=1, keepdims=True), (own, 128)),
        ],
        axis=1,
    )
    group_ref[...] = sums
    lines = sums_ref.shape[1]
    for step in range(n_cls):
        at = pl.multiple_of((cls ^ step) * lines, lines)
        sums_ref[step] = group_ref[pl.ds(at, lines), :]


def class_parts(own, n_cls, *operands):
    pooled, _, _, weight, _ = operands
    images, width = pooled.shape
    classes, embed = weight.shape
    return in_vmem(
        functools.partial(class_kernel, own),
        [
            f32(images, classes),
            f32(images, classes),
            f32(images, embed + 128),
            f32(n_cls, own // n_cls, 2 * embed + 256),
            f32(1, images),
        ],
        [
            pltpu.VMEM((own, classes), jnp.float32),
            pltpu.VMEM((own, 2 * embed + 256), jnp.float32),
        ],
        6,
        6 * images * embed * classes,
        operands,
    )


def aside_kernel(share, exp_ref, cos_ref, unit_ref, image_ref, weight_ref,
                 high_ref, low_ref, along_ref, unit_out, weight_out, marked_ref, mark_ref):
    images, classes = exp_ref.shape
    at = lax.axis_index("dp") * share
    block = pl.ds(pl.multiple_of(at // 128 * 128, 128), 128)
    take = one_hot(share, 128, lambda row: row + at % 128)
    high, low = split(unit_ref[:, block])
    unit = over_lanes(take, high) + over_lanes(take, low)
    unit_out[...] = unit
    weight_out[...] = over_lanes(take, weight_ref[:, block])
    marked = jnp.concatenate(split(unit * LOGIT_SCALE), axis=0)
    wide = 256
    for start in range(0, classes, wide):
        cols = pl.ds(start, wide)
        exponent, cosine = exp_ref[:, cols], cos_ref[:, cols]
        _, target = masks(image_ref, start, wide)
        high_ref[:, cols], low_ref[:, cols] = split(exponent)
        along_ref[:, cols] = exponent * cosine
        mark_ref[:, cols] = jnp.sum(jnp.where(target, LOGIT_SCALE * cosine, 0.0), axis=0, keepdims=True)
        both = jnp.dot(
            marked, jnp.where(target, 1.0, 0.0).astype(jnp.bfloat16), preferred_element_type=jnp.float32
        )
        marked_ref[:, cols] = both[:share] + both[share:]


def class_grad_aside(share, *operands):
    images, classes = operands[0].shape
    return in_vmem(
        functools.partial(aside_kernel, share),
        [
            jax.ShapeDtypeStruct((images, classes), jnp.bfloat16),
            jax.ShapeDtypeStruct((images, classes), jnp.bfloat16),
            f32(images, classes),
            f32(share, images),
            f32(share, classes),
            f32(share, classes),
            f32(1, classes),
        ],
        [],
        5,
        4 * images * share * classes,
        operands,
    )


def grad_kernel(total_ref, denom_ref, high_ref, low_ref, along_ref, unit_share_ref, weight_share_ref, marked_ref,
                mark_ref, scale_ref, unit_ref, grad_ref, loss_ref, embed_ref):
    images, classes = high_ref.shape
    share = unit_share_ref.shape[0]
    embed = embed_ref.shape[1]
    denom = denom_ref[...]
    ratio = jnp.where(denom > 0.0, LOGIT_SCALE / denom, 0.0)
    left = jnp.concatenate(split(unit_share_ref[...] * ratio), axis=0)
    column = jnp.broadcast_to(ratio, (128, images)).T[:, 0:1]
    dot = functools.partial(jnp.dot, preferred_element_type=jnp.float32)
    wide = 256
    for start in range(0, classes, wide):
        cols = pl.ds(start, wide)
        first = dot(left, high_ref[:, cols])
        grad = first[:share] + first[share:] + dot(left[:share], low_ref[:, cols]) - marked_ref[:, cols]
        along = jnp.sum(along_ref[:, cols] * column, axis=0, keepdims=True) - mark_ref[:, cols]
        scale = scale_ref[:, cols]
        grad_ref[:, cols] = (grad - weight_share_ref[:, cols] * (along * scale)) * scale

    lines = padded(embed_ref.shape[0])
    own = unit_ref[pl.ds(pl.multiple_of(lax.axis_index("cls") * lines, lines), lines), :][: embed_ref.shape[0]]
    total = total_ref[: embed_ref.shape[0], :]
    weighted, picked = total[:, :embed], total[:, embed : 2 * embed]
    own_denom, target_logit = total[:, 2 * embed : 2 * embed + 1], total[:, 2 * embed + 128 : 2 * embed + 129]
    loss = jnp.broadcast_to(jnp.log(own_denom) - target_logit, (loss_ref.shape[1], 128))
    loss = jnp.concatenate([loss, jnp.zeros((128 - loss_ref.shape[1], 128), jnp.float32)], axis=0)
    loss_ref[...] = loss.T[0:1, : loss_ref.shape[1]]
    unit_grad = LOGIT_SCALE * (weighted / own_denom - picked)
    own_unit = own[:, :embed]
    embed_ref[...] = (
        unit_grad - own_unit * jnp.sum(own_unit * unit_grad, axis=1, keepdims=True)
    ) / own[:, embed : embed + 1]


def class_grad_part(own_images, *operands):
    images, classes = operands[2].shape
    share = operands[5].shape[0]
    embed = operands[10].shape[1] - 128
    return in_vmem(
        grad_kernel,
        [f32(share, classes), f32(1, own_images), f32(own_images, embed)],
        [],
        5,
        6 * images * share * classes,
        operands,
    )


def per_device(
    attended,
    stream,
    out_proj,
    norm_gain,
    norm_shift,
    head_proj,
    class_weight,
    block_ids,
    block_count,
    labels,
):
    n_dp, n_cls = lax.axis_size("dp"), lax.axis_size("cls")
    n_z = n_dp // CORES
    dp, cls = lax.axis_index("dp"), lax.axis_index("cls")
    core = dp % CORES
    tokens, width = attended.shape
    images = tokens // P_SIZE
    size = n_cls * images
    lines = padded(images)
    group_lines = n_cls * lines
    rows = out_proj.shape[0]
    slice_rows = rows // n_cls
    slots = block_ids.shape[2]
    classes, embed = class_weight.shape

    facts = jnp.concatenate(
        [block_ids[0, 0], block_count[0], labels // BLOCK_ROWS, labels % BLOCK_ROWS]
    ).astype(jnp.bfloat16)
    n_facts = facts.shape[0]
    facts = jnp.pad(facts, (0, FACT_ROWS * embed - n_facts)).reshape(FACT_ROWS, embed)

    own_slice = lax.dynamic_slice_in_dim(out_proj, cls * slice_rows, slice_rows, 0)
    far = jnp.stack([z_swap(own_slice, step) for step in range(2, n_z)])
    near_from, _ = lax.optimization_barrier((out_proj, own_slice))
    near = z_swap(near_from, 1)
    own_other = core_swap(out_proj)
    far = after(far, own_other)
    head_rows = head_proj.shape[0]
    half = head_rows // 2
    head_half = lax.dynamic_slice_in_dim(head_proj, ((cls >> core) & 1) * half, half, 0)
    head_half = jnp.concatenate([head_half, facts], axis=0)
    from_plane = [plane_swap(far, step) for step in range(1, n_cls)]
    head_half = after(head_half, far)
    heads = [z_swap(head_half, step) for step in range(1, n_z)]
    near_other = core_swap(near)
    far = jnp.stack([far] + from_plane)
    if slice_rows % 16:
        ordered = jnp.zeros_like(far)
        for step in range(n_cls):
            ordered = lax.dynamic_update_index_in_dim(ordered, far[step], cls ^ step, 0)
        far = ordered.transpose(1, 0, 2, 3).reshape(1, n_z - 2, rows, width)
    far = after(far, near_other, heads[0])
    scale = lax.rsqrt(
        jnp.sum(jnp.square(class_weight.astype(jnp.float32)), axis=1) + NORM_EPSILON
    )[None, :]
    far_other = after(core_swap(far), scale)
    pooled = pool_tokens(
        attended, stream, out_proj, near, own_other, near_other, far, far_other, norm_gain.reshape(1, width), norm_shift.reshape(1, width)
    )

    column = jnp.stack([pooled] + [z_swap(pooled, step) for step in range(1, n_z)])
    heads[0] = after(heads[0], pooled)
    heads = jnp.stack([head_half] + heads)
    counterparts = half_swap(heads)

    groups = jnp.zeros((n_z, n_cls, lines, width), pooled.dtype)
    from_plane = [plane_swap(column, step) for step in range(1, n_cls)]
    for step, got in enumerate([column] + from_plane):
        groups = lax.dynamic_update_slice_in_dim(groups, got[:, None], cls ^ step, 1)
    counterparts = after(counterparts, from_plane[0])
    heads = jnp.concatenate([heads.reshape(-1, embed), counterparts.reshape(-1, embed)], axis=0)
    other_heads = core_swap(heads)
    total_lines = n_dp * group_lines
    whole_head, image_facts = group_facts(
        group_lines, slots, images, n_cls, classes, width, total_lines, heads, other_heads
    )
    groups = jnp.concatenate([groups, after(core_swap(groups), whole_head)], axis=0)
    pooled_all = groups.reshape(n_dp * group_lines, width)

    piece = group_lines * max(1, min(n_dp, 256 // group_lines))
    pieces = [slice(at, at + piece) for at in range(0, total_lines, piece)]
    parts = [
        class_parts(group_lines, n_cls, pooled_all[at], whole_head, image_facts[at], class_weight, scale)
        for at in pieces
    ]
    denoms = jnp.concatenate([p[4] for p in parts], axis=1)
    sums = parts[0][3]
    extra = -(-total_lines // sums.shape[2])
    denoms = jnp.pad(denoms, ((0, 0), (0, extra * sums.shape[2] - total_lines))).reshape(extra, -1)

    def packed(step):
        return jnp.concatenate([sums[step, :images], denoms], axis=0)

    total = packed(0)
    for step in range(n_cls - 1, 0, -1):
        total = total + plane_swap(packed(step), step)
    denominator = total[images:].reshape(1, -1)[:, :total_lines]
    share = embed // n_dp
    for k, (at, (exponent, cosine, unit, _, _)) in enumerate(zip(pieces, parts)):
        aside = class_grad_aside(share, exponent, cosine, unit, image_facts[at], class_weight)
        grad, loss, embed_part = class_grad_part(images, total, denominator[:, at], *aside, scale, unit)
        if k == 0:
            class_grad, sample_loss, embed_grad = grad, loss, embed_part
        else:
            class_grad = class_grad + grad
    return (sample_loss.reshape(images), embed_grad, class_grad.T)


def solution(mesh):
    placed = (
        P(("dp", "cls"), None),
        P(("dp", "cls"), None),
        P("dp", None),
        P(),
        P(),
        P("dp", None),
        P("cls", None),
        P("dp", "cls", None),
        P("dp", "cls"),
        P("dp"),
    )
    return jax.shard_map(
        per_device,
        mesh=mesh,
        in_specs=placed,
        out_specs=(P(("dp", "cls")), P(("dp", "cls"), None), P("cls", "dp")),
        check_vma=False,
    )
```

```python
import functools
import math

import jax
import jax.numpy as jnp
from jax import lax
from jax.experimental import pallas as pl
from jax.experimental.pallas import tpu as pltpu
from jax.sharding import PartitionSpec as P

P_SIZE = 144
BLOCK_ROWS = 128
CORES = 2
FACT_ROWS = 16

LOGIT_SCALE = 64.0
ANGLE_MARGIN = 0.5
NORM_EPSILON = 1e-06


def z_swap(value, step):
    count = lax.axis_size("dp")
    return lax.ppermute(value, "dp", [(i, i ^ (step * CORES)) for i in range(count)])


def core_swap(value):
    count = lax.axis_size("dp")
    return lax.ppermute(value, "dp", [(i, i ^ 1) for i in range(count)])


def half_swap(value):
    n_dp, n_cls = lax.axis_size("dp"), lax.axis_size("cls")
    pairs = [(dp * n_cls + c, dp * n_cls + (c ^ (1 << dp % CORES))) for dp in range(n_dp) for c in range(n_cls)]
    return lax.ppermute(value, ("dp", "cls"), pairs)


def plane_swap(value, step):
    count = lax.axis_size("cls")
    return lax.ppermute(value, "cls", [(i, i ^ step) for i in range(count)])


def pool_kernel(att_ref, stream_ref, own_ref, near_ref, own_other_ref, near_other_ref, far_ref, far_other_ref, gain_ref, shift_ref,
                out_ref, weight_ref, mixed_ref, pooled_ref):
    tokens, width = stream_ref.shape
    images = tokens // P_SIZE
    chunk = mixed_ref.shape[0]
    pieces = range(0, tokens, chunk)
    n_cls, n_far, slice_rows, _ = far_ref.shape
    rows = n_cls * slice_rows
    dp, cls = lax.axis_index("dp"), lax.axis_index("cls")
    z, core = dp // CORES, dp % CORES

    def place(shard, start, value):
        at = pl.multiple_of(shard * rows + start, slice_rows)
        weight_ref[pl.ds(at, value.shape[0]), :] = value

    for side, own, near, far in (
        (core, own_ref, near_ref, far_ref), (1 - core, own_other_ref, near_other_ref, far_other_ref)
    ):
        place(z * CORES + side, 0, own[...])
        place((z ^ 1) * CORES + side, 0, near[...])
        for k in range(n_far):
            for step in range(n_cls):
                start = (cls ^ step) * slice_rows if n_cls > 1 else 0
                place((z ^ (k + 2)) * CORES + side, start, far[step, k])
    step = 24
    for k, start in enumerate(pieces):
        mixed_ref[...] = jnp.dot(
            att_ref[pl.ds(start, chunk), :], weight_ref[...], preferred_element_type=jnp.float32
        )
        for image in range(chunk // P_SIZE):
            total = jnp.zeros((8, width), jnp.float32)
            for r in range(0, P_SIZE, step):
                at = image * P_SIZE + r
                x = mixed_ref[pl.ds(at, step), :] + stream_ref[pl.ds(start + at, step), :].astype(jnp.float32)
                centred = x - jnp.mean(x, axis=1, keepdims=True)
                variance = jnp.mean(centred * centred, axis=1, keepdims=True)
                scaled = centred * lax.rsqrt(variance + NORM_EPSILON)
                total = total + jnp.sum(scaled.reshape(step // 8, 8, width), axis=0)
            mean = jnp.sum(total, axis=0, keepdims=True) * (1.0 / P_SIZE)
            pooled_ref[pl.ds(start // P_SIZE + image, 1), :] = gain_ref[...] * mean + shift_ref[...]
    if images < pooled_ref.shape[0]:
        pooled_ref[images:, :] = jnp.zeros((pooled_ref.shape[0] - images, width), jnp.float32)
    out_ref[...] = pooled_ref[...].astype(out_ref.dtype)


def padded(images):
    return -(-images // 8) * 8


def after(value, *others):
    anywhere = pl.BlockSpec(memory_space=pl.ANY)
    return pl.pallas_call(
        lambda *refs: None,
        out_shape=jax.ShapeDtypeStruct(value.shape, value.dtype),
        in_specs=[anywhere] * (1 + len(others)),
        out_specs=anywhere,
        input_output_aliases={0: 0},
        compiler_params=pltpu.CompilerParams(vmem_limit_bytes=1024 * 1024),
    )(value, *others)


def in_vmem(kernel, outs, scratch, mib, flops, operands, in_hbm=0):
    vmem = pl.BlockSpec(memory_space=pltpu.VMEM)
    moved = sum(math.prod(x.shape) * x.dtype.itemsize for x in list(operands) + list(outs))
    return pl.pallas_call(
        kernel,
        out_shape=tuple(outs),
        in_specs=[pl.BlockSpec(memory_space=pl.ANY)] * in_hbm + [vmem] * (len(operands) - in_hbm),
        out_specs=(vmem,) * len(outs),
        scratch_shapes=scratch,
        compiler_params=pltpu.CompilerParams(vmem_limit_bytes=mib * 1024 * 1024),
        cost_estimate=pl.CostEstimate(flops=flops, bytes_accessed=moved, transcendentals=0),
    )(*operands)


def f32(*shape):
    return jax.ShapeDtypeStruct(shape, jnp.float32)


def pool_tokens(*operands):
    tokens, width = operands[0].shape
    images = tokens // P_SIZE
    lines = padded(images)
    chunk = (3 if images % 3 == 0 else 1) * P_SIZE
    return in_vmem(
        pool_kernel,
        [jax.ShapeDtypeStruct((lines, width), jnp.bfloat16)],
        [
            pltpu.VMEM((width, width), jnp.bfloat16),
            pltpu.VMEM((chunk, width), jnp.float32),
            pltpu.VMEM((lines, width), jnp.float32),
        ],
        12,
        2 * tokens * width * width,
        operands,
    )[0]


def split(value):
    high = value.astype(jnp.bfloat16)
    return high, (value - high.astype(jnp.float32)).astype(jnp.bfloat16)


def as_row(column):
    return jnp.broadcast_to(column, (column.shape[0], 128)).T[0:1]


def over_lanes(left, right):
    return lax.dot_general(left, right, (((1,), (1,)), ((), ())), preferred_element_type=jnp.float32)


def one_hot(rows, columns, at):
    row = lax.broadcasted_iota(jnp.int32, (rows, columns), 0)
    column = lax.broadcasted_iota(jnp.int32, (rows, columns), 1)
    return jnp.where(column == at(row), 1.0, 0.0).astype(jnp.bfloat16)


def masks(image_ref, start, wide):
    images = image_ref.shape[0]
    label, bits = image_ref[:, 0:1], image_ref[:, 1:2]
    live = [
        jnp.broadcast_to((bits & (1 << (k // BLOCK_ROWS))) != 0, (images, BLOCK_ROWS))
        for k in range(start, start + wide, BLOCK_ROWS)
    ]
    live = jnp.concatenate(live, axis=1)
    column = lax.broadcasted_iota(jnp.int32, (images, wide), 1) + start
    return live, live & (column == label)


def facts_kernel(own, slots, group_images, n_cls, classes, head_ref, other_ref, whole_ref, image_ref):
    width = whole_ref.shape[0]
    n_z = image_ref.shape[0] // (CORES * own)
    dp, cls = lax.axis_index("dp"), lax.axis_index("cls")
    z, core = dp // CORES, dp % CORES
    head_rows = width // (CORES * n_z)
    half = head_rows // 2
    block = half + FACT_ROWS
    size = group_images * n_cls
    lines = own // n_cls
    fact_lanes = -(-(slots + 1 + 2 * size) // 128) * 128
    row = lax.broadcasted_iota(jnp.int32, (own, fact_lanes), 0)
    lane = lax.broadcasted_iota(jnp.int32, (own, fact_lanes), 1)
    image = slots + 1 + row // lines * group_images + row % lines
    block_at = (lane == image) & (row % lines < group_images)
    row_at = (lane == image + size) & (row % lines < group_images)
    for side, source in ((core, head_ref), (1 - core, other_ref)):
        mine = (cls >> side) & 1
        for k in range(n_z):
            for part, which in ((0, mine), (1, 1 - mine)):
                at = pl.multiple_of(((z ^ k) * CORES + side) * head_rows + which * half, half)
                start = n_z * block + k * half if part else k * block
                whole_ref[pl.ds(at, half), :] = source[pl.ds(start, half), :]
    for which, source in enumerate((head_ref, other_ref)):
        for k in range(n_z):
            at = (which * n_z + k) * own
            facts = source[pl.ds(k * block + half, FACT_ROWS), :fact_lanes][0:1].astype(jnp.float32)
            everywhere = jnp.broadcast_to(facts, (own, fact_lanes))
            label = jnp.sum(
                jnp.where(block_at, everywhere * BLOCK_ROWS, jnp.where(row_at, everywhere, 0.0)), axis=1, keepdims=True
            ).astype(jnp.int32)
            bits = jnp.zeros((own, 1), jnp.int32)
            for slot in range(slots):
                used = facts[:, slots : slots + 1] > slot
                bits = bits + jnp.where(used, 1 << facts[:, slot : slot + 1].astype(jnp.int32), 0)
            bits = jnp.where(row[:, :1] % lines < group_images, bits, 0)
            image_ref[pl.ds(at, own), 0:1] = label - cls * classes
            image_ref[pl.ds(at, own), 1:2] = bits


def group_facts(own, slots, group_images, n_cls, classes, width, total, *operands):
    embed = operands[0].shape[1]
    return in_vmem(
        functools.partial(facts_kernel, own, slots, group_images, n_cls, classes),
        [jax.ShapeDtypeStruct((width, embed), jnp.bfloat16), jax.ShapeDtypeStruct((total, 2), jnp.int32)],
        [],
        4,
        0,
        operands,
    )


def class_kernel(own, pooled_ref, whole_ref, image_ref, weight_ref, scale_ref,
                 exp_ref, cos_ref, unit_ref, sums_ref, denom_ref, chosen_ref, group_ref):
    images = pooled_ref.shape[0]
    classes, embed = weight_ref.shape
    n_cls = sums_ref.shape[0]
    cls = lax.axis_index("cls")
    embedding = jnp.dot(pooled_ref[...], whole_ref[...], preferred_element_type=jnp.float32)
    norm = jnp.sqrt(jnp.sum(embedding * embedding, axis=1, keepdims=True) + NORM_EPSILON)
    unit = embedding * (1.0 / norm)
    unit_ref[:, :embed] = unit
    unit_ref[:, embed:] = jnp.broadcast_to(norm, (images, 128))
    terms = jnp.concatenate(split(unit), axis=0)
    denom = jnp.zeros((images, 128), jnp.float32)
    picked = jnp.zeros((own, 128), jnp.float32)
    wide = 256
    for start in range(0, classes, wide):
        cols = pl.ds(start, wide)
        both = over_lanes(terms, weight_ref[cols, :])
        cosine = (both[:images] + both[images:]) * scale_ref[:, cols]
        cos_ref[:, cols] = cosine
        live, target = masks(image_ref, start, wide)
        sine = jnp.sqrt(jnp.maximum(1.0 - cosine * cosine, 0.0))
        margin = cosine * math.cos(ANGLE_MARGIN) - sine * math.sin(ANGLE_MARGIN)
        logits = LOGIT_SCALE * jnp.where(target, margin, cosine)
        exponent = jnp.where(live, jnp.exp(logits), 0.0)
        exp_ref[:, cols] = exponent
        labelled = jnp.where(target, logits, 0.0)[:own]
        chosen_ref[:, cols] = jnp.where(target[:own], scale_ref[:, cols], 0.0)
        for k in range(0, wide, 128):
            denom = denom + exponent[:, k : k + 128]
            picked = picked + labelled[:, k : k + 128]
    denom = jnp.sum(denom, axis=1, keepdims=True)
    denom_ref[...] = as_row(denom)
    weighted = split(exp_ref[:own, :] * scale_ref[...])
    chosen = split(chosen_ref[...])
    sums = jnp.dot(
        jnp.concatenate(weighted + chosen, axis=0), weight_ref[...], preferred_element_type=jnp.float32
    )
    sums = jnp.concatenate(
        [
            sums[:own] + sums[own : 2 * own],
            sums[2 * own : 3 * own] + sums[3 * own :],
            jnp.broadcast_to(denom[:own], (own, 128)),
            jnp.broadcast_to(jnp.sum(picked, axis=1, keepdims=True), (own, 128)),
        ],
        axis=1,
    )
    group_ref[...] = sums
    lines = sums_ref.shape[1]
    for step in range(n_cls):
        at = pl.multiple_of((cls ^ step) * lines, lines)
        sums_ref[step] = group_ref[pl.ds(at, lines), :]


def class_parts(own, n_cls, *operands):
    pooled, _, _, weight, _ = operands
    images, width = pooled.shape
    classes, embed = weight.shape
    return in_vmem(
        functools.partial(class_kernel, own),
        [
            f32(images, classes),
            f32(images, classes),
            f32(images, embed + 128),
            f32(n_cls, own // n_cls, 2 * embed + 256),
            f32(1, images),
        ],
        [
            pltpu.VMEM((own, classes), jnp.float32),
            pltpu.VMEM((own, 2 * embed + 256), jnp.float32),
        ],
        6,
        6 * images * embed * classes,
        operands,
    )


def aside_kernel(share, exp_ref, cos_ref, unit_ref, image_ref, weight_ref,
                 high_ref, low_ref, along_ref, unit_out, weight_out, marked_ref, mark_ref):
    images, classes = exp_ref.shape
    at = lax.axis_index("dp") * share
    block = pl.ds(pl.multiple_of(at // 128 * 128, 128), 128)
    take = one_hot(share, 128, lambda row: row + at % 128)
    high, low = split(unit_ref[:, block])
    unit = over_lanes(take, high) + over_lanes(take, low)
    unit_out[...] = unit
    weight_out[...] = over_lanes(take, weight_ref[:, block])
    marked = jnp.concatenate(split(unit * LOGIT_SCALE), axis=0)
    wide = 256
    for start in range(0, classes, wide):
        cols = pl.ds(start, wide)
        exponent, cosine = exp_ref[:, cols], cos_ref[:, cols]
        _, target = masks(image_ref, start, wide)
        high_ref[:, cols], low_ref[:, cols] = split(exponent)
        along_ref[:, cols] = exponent * cosine
        mark_ref[:, cols] = jnp.sum(jnp.where(target, LOGIT_SCALE * cosine, 0.0), axis=0, keepdims=True)
        both = jnp.dot(
            marked, jnp.where(target, 1.0, 0.0).astype(jnp.bfloat16), preferred_element_type=jnp.float32
        )
        marked_ref[:, cols] = both[:share] + both[share:]


def class_grad_aside(share, *operands):
    images, classes = operands[0].shape
    return in_vmem(
        functools.partial(aside_kernel, share),
        [
            jax.ShapeDtypeStruct((images, classes), jnp.bfloat16),
            jax.ShapeDtypeStruct((images, classes), jnp.bfloat16),
            f32(images, classes),
            f32(share, images),
            f32(share, classes),
            f32(share, classes),
            f32(1, classes),
        ],
        [],
        5,
        4 * images * share * classes,
        operands,
    )


def grad_kernel(total_ref, denom_ref, high_ref, low_ref, along_ref, unit_share_ref, weight_share_ref, marked_ref,
                mark_ref, scale_ref, unit_ref, grad_ref, loss_ref, embed_ref):
    images, classes = high_ref.shape
    share = unit_share_ref.shape[0]
    embed = embed_ref.shape[1]
    denom = denom_ref[...]
    ratio = jnp.where(denom > 0.0, LOGIT_SCALE / denom, 0.0)
    left = jnp.concatenate(split(unit_share_ref[...] * ratio), axis=0)
    column = jnp.broadcast_to(ratio, (128, images)).T[:, 0:1]
    dot = functools.partial(jnp.dot, preferred_element_type=jnp.float32)
    wide = 256
    for start in range(0, classes, wide):
        cols = pl.ds(start, wide)
        first = dot(left, high_ref[:, cols])
        grad = first[:share] + first[share:] + dot(left[:share], low_ref[:, cols]) - marked_ref[:, cols]
        along = jnp.sum(along_ref[:, cols] * column, axis=0, keepdims=True) - mark_ref[:, cols]
        scale = scale_ref[:, cols]
        grad_ref[:, cols] = (grad - weight_share_ref[:, cols] * (along * scale)) * scale

    lines = padded(embed_ref.shape[0])
    own = unit_ref[pl.ds(pl.multiple_of(lax.axis_index("cls") * lines, lines), lines), :][: embed_ref.shape[0]]
    total = total_ref[: embed_ref.shape[0], :]
    weighted, picked = total[:, :embed], total[:, embed : 2 * embed]
    own_denom, target_logit = total[:, 2 * embed : 2 * embed + 1], total[:, 2 * embed + 128 : 2 * embed + 129]
    loss = jnp.broadcast_to(jnp.log(own_denom) - target_logit, (loss_ref.shape[1], 128))
    loss = jnp.concatenate([loss, jnp.zeros((128 - loss_ref.shape[1], 128), jnp.float32)], axis=0)
    loss_ref[...] = loss.T[0:1, : loss_ref.shape[1]]
    unit_grad = LOGIT_SCALE * (weighted / own_denom - picked)
    own_unit = own[:, :embed]
    embed_ref[...] = (
        unit_grad - own_unit * jnp.sum(own_unit * unit_grad, axis=1, keepdims=True)
    ) / own[:, embed : embed + 1]


def class_grad_part(own_images, *operands):
    images, classes = operands[2].shape
    share = operands[5].shape[0]
    embed = operands[10].shape[1] - 128
    return in_vmem(
        grad_kernel,
        [f32(share, classes), f32(1, own_images), f32(own_images, embed)],
        [],
        5,
        6 * images * share * classes,
        operands,
    )


def per_device(
    attended,
    stream,
    out_proj,
    norm_gain,
    norm_shift,
    head_proj,
    class_weight,
    block_ids,
    block_count,
    labels,
):
    n_dp, n_cls = lax.axis_size("dp"), lax.axis_size("cls")
    n_z = n_dp // CORES
    dp, cls = lax.axis_index("dp"), lax.axis_index("cls")
    core = dp % CORES
    tokens, width = attended.shape
    images = tokens // P_SIZE
    size = n_cls * images
    lines = padded(images)
    group_lines = n_cls * lines
    rows = out_proj.shape[0]
    slice_rows = rows // n_cls
    slots = block_ids.shape[2]
    classes, embed = class_weight.shape

    facts = jnp.concatenate(
        [block_ids[0, 0], block_count[0], labels // BLOCK_ROWS, labels % BLOCK_ROWS]
    ).astype(jnp.bfloat16)
    n_facts = facts.shape[0]
    facts = jnp.pad(facts, (0, FACT_ROWS * embed - n_facts)).reshape(FACT_ROWS, embed)

    own_slice = lax.dynamic_slice_in_dim(out_proj, cls * slice_rows, slice_rows, 0)
    far = jnp.stack([z_swap(own_slice, step) for step in range(2, n_z)])
    near_from, _ = lax.optimization_barrier((out_proj, own_slice))
    near = z_swap(near_from, 1)
    own_other = core_swap(out_proj)
    far = after(far, own_other)
    head_rows = head_proj.shape[0]
    half = head_rows // 2
    head_half = lax.dynamic_slice_in_dim(head_proj, ((cls >> core) & 1) * half, half, 0)
    head_half = jnp.concatenate([head_half, facts], axis=0)
    from_plane = [plane_swap(far, step) for step in range(1, n_cls)]
    head_half = after(head_half, far)
    heads = [z_swap(head_half, step) for step in range(1, n_z)]
    near_other = core_swap(near)
    far = jnp.stack([far] + from_plane)
    if slice_rows % 16:
        ordered = jnp.zeros_like(far)
        for step in range(n_cls):
            ordered = lax.dynamic_update_index_in_dim(ordered, far[step], cls ^ step, 0)
        far = ordered.transpose(1, 0, 2, 3).reshape(1, n_z - 2, rows, width)
    far = after(far, near_other, heads[0])
    scale = lax.rsqrt(
        jnp.sum(jnp.square(class_weight.astype(jnp.float32)), axis=1) + NORM_EPSILON
    )[None, :]
    far_other = after(core_swap(far), scale)
    pooled = pool_tokens(
        attended, stream, out_proj, near, own_other, near_other, far, far_other, norm_gain.reshape(1, width), norm_shift.reshape(1, width)
    )

    column = jnp.stack([pooled] + [z_swap(pooled, step) for step in range(1, n_z)])
    heads = [after(rows_of, pooled) for rows_of in heads]
    counterparts = half_swap(jnp.stack([rows_of[:half] for rows_of in heads]))
    heads = jnp.stack([head_half] + heads)

    groups = jnp.zeros((n_z, n_cls, lines, width), pooled.dtype)
    from_plane = [plane_swap(column, step) for step in range(1, n_cls)]
    for step, got in enumerate([column] + from_plane):
        groups = lax.dynamic_update_slice_in_dim(groups, got[:, None], cls ^ step, 1)
    counterparts = after(counterparts, from_plane[0])
    own_counterpart = lax.dynamic_slice_in_dim(head_proj, (1 - ((cls >> core) & 1)) * half, half, 0)
    heads = jnp.concatenate([heads.reshape(-1, embed), own_counterpart, counterparts.reshape(-1, embed)], axis=0)
    other_heads = core_swap(heads)
    total_lines = n_dp * group_lines
    whole_head, image_facts = group_facts(
        group_lines, slots, images, n_cls, classes, width, total_lines, heads, other_heads
    )
    groups = jnp.concatenate([groups, after(core_swap(groups), whole_head)], axis=0)
    pooled_all = groups.reshape(n_dp * group_lines, width)

    piece = group_lines * max(1, min(n_dp, 256 // group_lines))
    pieces = [slice(at, at + piece) for at in range(0, total_lines, piece)]
    parts = [
        class_parts(group_lines, n_cls, pooled_all[at], whole_head, image_facts[at], class_weight, scale)
        for at in pieces
    ]
    denoms = jnp.concatenate([p[4] for p in parts], axis=1)
    sums = parts[0][3]
    extra = -(-total_lines // sums.shape[2])
    denoms = jnp.pad(denoms, ((0, 0), (0, extra * sums.shape[2] - total_lines))).reshape(extra, -1)

    def packed(step):
        return jnp.concatenate([sums[step, :images], denoms], axis=0)

    total = packed(0)
    for step in range(n_cls - 1, 0, -1):
        total = total + plane_swap(packed(step), step)
    denominator = total[images:].reshape(1, -1)[:, :total_lines]
    share = embed // n_dp
    for k, (at, (exponent, cosine, unit, _, _)) in enumerate(zip(pieces, parts)):
        aside = class_grad_aside(share, exponent, cosine, unit, image_facts[at], class_weight)
        grad, loss, embed_part = class_grad_part(images, total, denominator[:, at], *aside, scale, unit)
        if k == 0:
            class_grad, sample_loss, embed_grad = grad, loss, embed_part
        else:
            class_grad = class_grad + grad
    return (sample_loss.reshape(images), embed_grad, class_grad.T)


def solution(mesh):
    placed = (
        P(("dp", "cls"), None),
        P(("dp", "cls"), None),
        P("dp", None),
        P(),
        P(),
        P("dp", None),
        P("cls", None),
        P("dp", "cls", None),
        P("dp", "cls"),
        P("dp"),
    )
    return jax.shard_map(
        per_device,
        mesh=mesh,
        in_specs=placed,
        out_specs=(P(("dp", "cls")), P(("dp", "cls"), None), P("cls", "dp")),
        check_vma=False,
    )
```

```python
import functools
import math

import jax
import jax.numpy as jnp
from jax import lax
from jax.experimental import pallas as pl
from jax.experimental.pallas import tpu as pltpu
from jax.sharding import PartitionSpec as P

P_SIZE = 144
BLOCK_ROWS = 128
CORES = 2
FACT_ROWS = 16

LOGIT_SCALE = 64.0
ANGLE_MARGIN = 0.5
NORM_EPSILON = 1e-06


def z_swap(value, step):
    count = lax.axis_size("dp")
    return lax.ppermute(value, "dp", [(i, i ^ (step * CORES)) for i in range(count)])


def core_swap(value):
    count = lax.axis_size("dp")
    return lax.ppermute(value, "dp", [(i, i ^ 1) for i in range(count)])


def half_swap(value):
    n_dp, n_cls = lax.axis_size("dp"), lax.axis_size("cls")
    pairs = [(dp * n_cls + c, dp * n_cls + (c ^ (1 << dp % CORES))) for dp in range(n_dp) for c in range(n_cls)]
    return lax.ppermute(value, ("dp", "cls"), pairs)


def plane_swap(value, step):
    count = lax.axis_size("cls")
    return lax.ppermute(value, "cls", [(i, i ^ step) for i in range(count)])


def pool_kernel(att_ref, stream_ref, own_ref, near_ref, own_other_ref, near_other_ref, far_ref, far_other_ref, gain_ref, shift_ref,
                out_ref, weight_ref, mixed_ref, pooled_ref):
    tokens, width = stream_ref.shape
    images = tokens // P_SIZE
    chunk = mixed_ref.shape[0]
    pieces = range(0, tokens, chunk)
    n_cls, n_far, slice_rows, _ = far_ref.shape
    rows = n_cls * slice_rows
    dp, cls = lax.axis_index("dp"), lax.axis_index("cls")
    z, core = dp // CORES, dp % CORES

    def place(shard, start, value):
        at = pl.multiple_of(shard * rows + start, slice_rows)
        weight_ref[pl.ds(at, value.shape[0]), :] = value

    for side, own, near, far in (
        (core, own_ref, near_ref, far_ref), (1 - core, own_other_ref, near_other_ref, far_other_ref)
    ):
        place(z * CORES + side, 0, own[...])
        place((z ^ 1) * CORES + side, 0, near[...])
        for k in range(n_far):
            for step in range(n_cls):
                start = (cls ^ step) * slice_rows if n_cls > 1 else 0
                place((z ^ (k + 2)) * CORES + side, start, far[step, k])
    step = 24
    for k, start in enumerate(pieces):
        mixed_ref[...] = jnp.dot(
            att_ref[pl.ds(start, chunk), :], weight_ref[...], preferred_element_type=jnp.float32
        )
        for image in range(chunk // P_SIZE):
            total = jnp.zeros((8, width), jnp.float32)
            for r in range(0, P_SIZE, step):
                at = image * P_SIZE + r
                x = mixed_ref[pl.ds(at, step), :] + stream_ref[pl.ds(start + at, step), :].astype(jnp.float32)
                centred = x - jnp.mean(x, axis=1, keepdims=True)
                variance = jnp.mean(centred * centred, axis=1, keepdims=True)
                scaled = centred * lax.rsqrt(variance + NORM_EPSILON)
                total = total + jnp.sum(scaled.reshape(step // 8, 8, width), axis=0)
            mean = jnp.sum(total, axis=0, keepdims=True) * (1.0 / P_SIZE)
            pooled_ref[pl.ds(start // P_SIZE + image, 1), :] = gain_ref[...] * mean + shift_ref[...]
    if images < pooled_ref.shape[0]:
        pooled_ref[images:, :] = jnp.zeros((pooled_ref.shape[0] - images, width), jnp.float32)
    out_ref[...] = pooled_ref[...].astype(out_ref.dtype)


def padded(images):
    return -(-images // 8) * 8


def after(value, *others):
    anywhere = pl.BlockSpec(memory_space=pl.ANY)
    return pl.pallas_call(
        lambda *refs: None,
        out_shape=jax.ShapeDtypeStruct(value.shape, value.dtype),
        in_specs=[anywhere] * (1 + len(others)),
        out_specs=anywhere,
        input_output_aliases={0: 0},
        compiler_params=pltpu.CompilerParams(vmem_limit_bytes=1024 * 1024),
    )(value, *others)


def in_vmem(kernel, outs, scratch, mib, flops, operands, in_hbm=0):
    vmem = pl.BlockSpec(memory_space=pltpu.VMEM)
    moved = sum(math.prod(x.shape) * x.dtype.itemsize for x in list(operands) + list(outs))
    return pl.pallas_call(
        kernel,
        out_shape=tuple(outs),
        in_specs=[pl.BlockSpec(memory_space=pl.ANY)] * in_hbm + [vmem] * (len(operands) - in_hbm),
        out_specs=(vmem,) * len(outs),
        scratch_shapes=scratch,
        compiler_params=pltpu.CompilerParams(vmem_limit_bytes=mib * 1024 * 1024),
        cost_estimate=pl.CostEstimate(flops=flops, bytes_accessed=moved, transcendentals=0),
    )(*operands)


def f32(*shape):
    return jax.ShapeDtypeStruct(shape, jnp.float32)


def pool_tokens(*operands):
    tokens, width = operands[0].shape
    images = tokens // P_SIZE
    lines = padded(images)
    chunk = (3 if images % 3 == 0 else 1) * P_SIZE
    return in_vmem(
        pool_kernel,
        [jax.ShapeDtypeStruct((lines, width), jnp.bfloat16)],
        [
            pltpu.VMEM((width, width), jnp.bfloat16),
            pltpu.VMEM((chunk, width), jnp.float32),
            pltpu.VMEM((lines, width), jnp.float32),
        ],
        12,
        2 * tokens * width * width,
        operands,
    )[0]


def split(value):
    high = value.astype(jnp.bfloat16)
    return high, (value - high.astype(jnp.float32)).astype(jnp.bfloat16)


def as_row(column):
    return jnp.broadcast_to(column, (column.shape[0], 128)).T[0:1]


def over_lanes(left, right):
    return lax.dot_general(left, right, (((1,), (1,)), ((), ())), preferred_element_type=jnp.float32)


def one_hot(rows, columns, at):
    row = lax.broadcasted_iota(jnp.int32, (rows, columns), 0)
    column = lax.broadcasted_iota(jnp.int32, (rows, columns), 1)
    return jnp.where(column == at(row), 1.0, 0.0).astype(jnp.bfloat16)


def masks(image_ref, start, wide):
    images = image_ref.shape[0]
    label, bits = image_ref[:, 0:1], image_ref[:, 1:2]
    live = [
        jnp.broadcast_to((bits & (1 << (k // BLOCK_ROWS))) != 0, (images, BLOCK_ROWS))
        for k in range(start, start + wide, BLOCK_ROWS)
    ]
    live = jnp.concatenate(live, axis=1)
    column = lax.broadcasted_iota(jnp.int32, (images, wide), 1) + start
    return live, live & (column == label)


def facts_kernel(own, slots, group_images, n_cls, classes, head_ref, other_ref, whole_ref, image_ref):
    width = whole_ref.shape[0]
    n_z = image_ref.shape[0] // (CORES * own)
    dp, cls = lax.axis_index("dp"), lax.axis_index("cls")
    z, core = dp // CORES, dp % CORES
    head_rows = width // (CORES * n_z)
    half = head_rows // 2
    block = half + FACT_ROWS
    size = group_images * n_cls
    lines = own // n_cls
    fact_lanes = -(-(slots + 1 + 2 * size) // 128) * 128
    row = lax.broadcasted_iota(jnp.int32, (own, fact_lanes), 0)
    lane = lax.broadcasted_iota(jnp.int32, (own, fact_lanes), 1)
    image = slots + 1 + row // lines * group_images + row % lines
    block_at = (lane == image) & (row % lines < group_images)
    row_at = (lane == image + size) & (row % lines < group_images)
    for side, source in ((core, head_ref), (1 - core, other_ref)):
        mine = (cls >> side) & 1
        for k in range(n_z):
            for part, which in ((0, mine), (1, 1 - mine)):
                at = pl.multiple_of(((z ^ k) * CORES + side) * head_rows + which * half, half)
                start = n_z * block + k * half if part else k * block
                whole_ref[pl.ds(at, half), :] = source[pl.ds(start, half), :]
    for which, source in enumerate((head_ref, other_ref)):
        for k in range(n_z):
            at = (which * n_z + k) * own
            facts = source[pl.ds(k * block + half, FACT_ROWS), :fact_lanes][0:1].astype(jnp.float32)
            everywhere = jnp.broadcast_to(facts, (own, fact_lanes))
            label = jnp.sum(
                jnp.where(block_at, everywhere * BLOCK_ROWS, jnp.where(row_at, everywhere, 0.0)), axis=1, keepdims=True
            ).astype(jnp.int32)
            bits = jnp.zeros((own, 1), jnp.int32)
            for slot in range(slots):
                used = facts[:, slots : slots + 1] > slot
                bits = bits + jnp.where(used, 1 << facts[:, slot : slot + 1].astype(jnp.int32), 0)
            bits = jnp.where(row[:, :1] % lines < group_images, bits, 0)
            image_ref[pl.ds(at, own), 0:1] = label - cls * classes
            image_ref[pl.ds(at, own), 1:2] = bits


def group_facts(own, slots, group_images, n_cls, classes, width, total, *operands):
    embed = operands[0].shape[1]
    return in_vmem(
        functools.partial(facts_kernel, own, slots, group_images, n_cls, classes),
        [jax.ShapeDtypeStruct((width, embed), jnp.bfloat16), jax.ShapeDtypeStruct((total, 2), jnp.int32)],
        [],
        4,
        0,
        operands,
    )


def class_kernel(own, pooled_ref, whole_ref, image_ref, weight_ref, scale_ref,
                 exp_ref, cos_ref, unit_ref, sums_ref, denom_ref, chosen_ref, group_ref):
    images = pooled_ref.shape[0]
    classes, embed = weight_ref.shape
    n_cls = sums_ref.shape[0]
    cls = lax.axis_index("cls")
    embedding = jnp.dot(pooled_ref[...], whole_ref[...], preferred_element_type=jnp.float32)
    norm = jnp.sqrt(jnp.sum(embedding * embedding, axis=1, keepdims=True) + NORM_EPSILON)
    unit = embedding * (1.0 / norm)
    unit_ref[:, :embed] = unit
    unit_ref[:, embed:] = jnp.broadcast_to(norm, (images, 128))
    terms = jnp.concatenate(split(unit), axis=0)
    denom = jnp.zeros((images, 128), jnp.float32)
    picked = jnp.zeros((own, 128), jnp.float32)
    wide = 256
    for start in range(0, classes, wide):
        cols = pl.ds(start, wide)
        both = over_lanes(terms, weight_ref[cols, :])
        cosine = (both[:images] + both[images:]) * scale_ref[:, cols]
        cos_ref[:, cols] = cosine
        live, target = masks(image_ref, start, wide)
        sine = jnp.sqrt(jnp.maximum(1.0 - cosine * cosine, 0.0))
        margin = cosine * math.cos(ANGLE_MARGIN) - sine * math.sin(ANGLE_MARGIN)
        logits = LOGIT_SCALE * jnp.where(target, margin, cosine)
        exponent = jnp.where(live, jnp.exp(logits), 0.0)
        exp_ref[:, cols] = exponent
        labelled = jnp.where(target, logits, 0.0)[:own]
        chosen_ref[:, cols] = jnp.where(target[:own], scale_ref[:, cols], 0.0)
        for k in range(0, wide, 128):
            denom = denom + exponent[:, k : k + 128]
            picked = picked + labelled[:, k : k + 128]
    denom = jnp.sum(denom, axis=1, keepdims=True)
    denom_ref[...] = as_row(denom)
    weighted = split(exp_ref[:own, :] * scale_ref[...])
    chosen = split(chosen_ref[...])
    sums = jnp.dot(
        jnp.concatenate(weighted + chosen, axis=0), weight_ref[...], preferred_element_type=jnp.float32
    )
    sums = jnp.concatenate(
        [
            sums[:own] + sums[own : 2 * own],
            sums[2 * own : 3 * own] + sums[3 * own :],
            jnp.where(
                lax.broadcasted_iota(jnp.int32, (own, 128), 1) < 64,
                denom[:own],
                jnp.sum(picked, axis=1, keepdims=True),
            ),
        ],
        axis=1,
    )
    group_ref[...] = sums
    lines = sums_ref.shape[1]
    for step in range(n_cls):
        at = pl.multiple_of((cls ^ step) * lines, lines)
        sums_ref[step] = group_ref[pl.ds(at, lines), :]


def class_parts(own, n_cls, *operands):
    pooled, _, _, weight, _ = operands
    images, width = pooled.shape
    classes, embed = weight.shape
    return in_vmem(
        functools.partial(class_kernel, own),
        [
            f32(images, classes),
            f32(images, classes),
            f32(images, embed + 128),
            f32(n_cls, own // n_cls, 2 * embed + 128),
            f32(1, images),
        ],
        [
            pltpu.VMEM((own, classes), jnp.float32),
            pltpu.VMEM((own, 2 * embed + 128), jnp.float32),
        ],
        6,
        6 * images * embed * classes,
        operands,
    )


def aside_kernel(share, exp_ref, cos_ref, unit_ref, image_ref, weight_ref,
                 high_ref, low_ref, along_ref, unit_out, weight_out, marked_ref, mark_ref):
    images, classes = exp_ref.shape
    at = lax.axis_index("dp") * share
    block = pl.ds(pl.multiple_of(at // 128 * 128, 128), 128)
    take = one_hot(share, 128, lambda row: row + at % 128)
    high, low = split(unit_ref[:, block])
    unit = over_lanes(take, high) + over_lanes(take, low)
    unit_out[...] = unit
    weight_out[...] = over_lanes(take, weight_ref[:, block])
    marked = jnp.concatenate(split(unit * LOGIT_SCALE), axis=0)
    wide = 256
    for start in range(0, classes, wide):
        cols = pl.ds(start, wide)
        exponent, cosine = exp_ref[:, cols], cos_ref[:, cols]
        _, target = masks(image_ref, start, wide)
        high_ref[:, cols], low_ref[:, cols] = split(exponent)
        along_ref[:, cols] = exponent * cosine
        mark_ref[:, cols] = jnp.sum(jnp.where(target, LOGIT_SCALE * cosine, 0.0), axis=0, keepdims=True)
        both = jnp.dot(
            marked, jnp.where(target, 1.0, 0.0).astype(jnp.bfloat16), preferred_element_type=jnp.float32
        )
        marked_ref[:, cols] = both[:share] + both[share:]


def class_grad_aside(share, *operands):
    images, classes = operands[0].shape
    return in_vmem(
        functools.partial(aside_kernel, share),
        [
            jax.ShapeDtypeStruct((images, classes), jnp.bfloat16),
            jax.ShapeDtypeStruct((images, classes), jnp.bfloat16),
            f32(images, classes),
            f32(share, images),
            f32(share, classes),
            f32(share, classes),
            f32(1, classes),
        ],
        [],
        5,
        4 * images * share * classes,
        operands,
    )


def grad_kernel(total_ref, denom_ref, high_ref, low_ref, along_ref, unit_share_ref, weight_share_ref, marked_ref,
                mark_ref, scale_ref, unit_ref, grad_ref, loss_ref, embed_ref):
    images, classes = high_ref.shape
    share = unit_share_ref.shape[0]
    embed = embed_ref.shape[1]
    denom = denom_ref[...]
    ratio = jnp.where(denom > 0.0, LOGIT_SCALE / denom, 0.0)
    left = jnp.concatenate(split(unit_share_ref[...] * ratio), axis=0)
    column = jnp.broadcast_to(ratio, (128, images)).T[:, 0:1]
    dot = functools.partial(jnp.dot, preferred_element_type=jnp.float32)
    wide = 256
    for start in range(0, classes, wide):
        cols = pl.ds(start, wide)
        first = dot(left, high_ref[:, cols])
        grad = first[:share] + first[share:] + dot(left[:share], low_ref[:, cols]) - marked_ref[:, cols]
        along = jnp.sum(along_ref[:, cols] * column, axis=0, keepdims=True) - mark_ref[:, cols]
        scale = scale_ref[:, cols]
        grad_ref[:, cols] = (grad - weight_share_ref[:, cols] * (along * scale)) * scale

    lines = padded(embed_ref.shape[0])
    own = unit_ref[pl.ds(pl.multiple_of(lax.axis_index("cls") * lines, lines), lines), :][: embed_ref.shape[0]]
    total = total_ref[: embed_ref.shape[0], :]
    weighted, picked = total[:, :embed], total[:, embed : 2 * embed]
    own_denom, target_logit = total[:, 2 * embed : 2 * embed + 1], total[:, 2 * embed + 64 : 2 * embed + 65]
    loss = jnp.broadcast_to(jnp.log(own_denom) - target_logit, (loss_ref.shape[1], 128))
    loss = jnp.concatenate([loss, jnp.zeros((128 - loss_ref.shape[1], 128), jnp.float32)], axis=0)
    loss_ref[...] = loss.T[0:1, : loss_ref.shape[1]]
    unit_grad = LOGIT_SCALE * (weighted / own_denom - picked)
    own_unit = own[:, :embed]
    embed_ref[...] = (
        unit_grad - own_unit * jnp.sum(own_unit * unit_grad, axis=1, keepdims=True)
    ) / own[:, embed : embed + 1]


def class_grad_part(own_images, *operands):
    images, classes = operands[2].shape
    share = operands[5].shape[0]
    embed = operands[10].shape[1] - 128
    return in_vmem(
        grad_kernel,
        [f32(share, classes), f32(1, own_images), f32(own_images, embed)],
        [],
        5,
        6 * images * share * classes,
        operands,
    )


def per_device(
    attended,
    stream,
    out_proj,
    norm_gain,
    norm_shift,
    head_proj,
    class_weight,
    block_ids,
    block_count,
    labels,
):
    n_dp, n_cls = lax.axis_size("dp"), lax.axis_size("cls")
    n_z = n_dp // CORES
    dp, cls = lax.axis_index("dp"), lax.axis_index("cls")
    core = dp % CORES
    tokens, width = attended.shape
    images = tokens // P_SIZE
    size = n_cls * images
    lines = padded(images)
    group_lines = n_cls * lines
    rows = out_proj.shape[0]
    slice_rows = rows // n_cls
    slots = block_ids.shape[2]
    classes, embed = class_weight.shape

    facts = jnp.concatenate(
        [block_ids[0, 0], block_count[0], labels // BLOCK_ROWS, labels % BLOCK_ROWS]
    ).astype(jnp.bfloat16)
    n_facts = facts.shape[0]
    facts = jnp.pad(facts, (0, FACT_ROWS * embed - n_facts)).reshape(FACT_ROWS, embed)

    own_slice = lax.dynamic_slice_in_dim(out_proj, cls * slice_rows, slice_rows, 0)
    far = jnp.stack([z_swap(own_slice, step) for step in range(2, n_z)])
    near_from, _ = lax.optimization_barrier((out_proj, own_slice))
    near = z_swap(near_from, 1)
    own_other = core_swap(out_proj)
    far = after(far, own_other)
    head_rows = head_proj.shape[0]
    half = head_rows // 2
    head_half = lax.dynamic_slice_in_dim(head_proj, ((cls >> core) & 1) * half, half, 0)
    head_half = jnp.concatenate([head_half, facts], axis=0)
    from_plane = [plane_swap(far, step) for step in range(1, n_cls)]
    head_half = after(head_half, far)
    heads = [z_swap(head_half, step) for step in range(1, n_z)]
    near_other = core_swap(near)
    far = jnp.stack([far] + from_plane)
    if slice_rows % 16:
        ordered = jnp.zeros_like(far)
        for step in range(n_cls):
            ordered = lax.dynamic_update_index_in_dim(ordered, far[step], cls ^ step, 0)
        far = ordered.transpose(1, 0, 2, 3).reshape(1, n_z - 2, rows, width)
    far = after(far, near_other, heads[0])
    scale = lax.rsqrt(
        jnp.sum(jnp.square(class_weight.astype(jnp.float32)), axis=1) + NORM_EPSILON
    )[None, :]
    far_other = after(core_swap(far), scale)
    pooled = pool_tokens(
        attended, stream, out_proj, near, own_other, near_other, far, far_other, norm_gain.reshape(1, width), norm_shift.reshape(1, width)
    )

    column = jnp.stack([pooled] + [z_swap(pooled, step) for step in range(1, n_z)])
    heads = [after(rows_of, pooled) for rows_of in heads]
    counterparts = half_swap(jnp.stack([rows_of[:half] for rows_of in heads]))
    heads = jnp.stack([head_half] + heads)

    groups = jnp.zeros((n_z, n_cls, lines, width), pooled.dtype)
    from_plane = [plane_swap(column, step) for step in range(1, n_cls)]
    for step, got in enumerate([column] + from_plane):
        groups = lax.dynamic_update_slice_in_dim(groups, got[:, None], cls ^ step, 1)
    counterparts = after(counterparts, from_plane[0])
    own_counterpart = lax.dynamic_slice_in_dim(head_proj, (1 - ((cls >> core) & 1)) * half, half, 0)
    heads = jnp.concatenate([heads.reshape(-1, embed), own_counterpart, counterparts.reshape(-1, embed)], axis=0)
    other_heads = core_swap(heads)
    total_lines = n_dp * group_lines
    whole_head, image_facts = group_facts(
        group_lines, slots, images, n_cls, classes, width, total_lines, heads, other_heads
    )
    groups = jnp.concatenate([groups, after(core_swap(groups), whole_head)], axis=0)
    pooled_all = groups.reshape(n_dp * group_lines, width)

    piece = group_lines * max(1, min(n_dp, 256 // group_lines))
    pieces = [slice(at, at + piece) for at in range(0, total_lines, piece)]
    parts = [
        class_parts(group_lines, n_cls, pooled_all[at], whole_head, image_facts[at], class_weight, scale)
        for at in pieces
    ]
    denoms = jnp.concatenate([p[4] for p in parts], axis=1)
    sums = parts[0][3]
    extra = -(-total_lines // sums.shape[2])
    denoms = jnp.pad(denoms, ((0, 0), (0, extra * sums.shape[2] - total_lines))).reshape(extra, -1)

    def packed(step):
        return jnp.concatenate([sums[step, :images], denoms], axis=0)

    total = packed(0)
    for step in range(n_cls - 1, 0, -1):
        total = total + plane_swap(packed(step), step)
    denominator = total[images:].reshape(1, -1)[:, :total_lines]
    share = embed // n_dp
    for k, (at, (exponent, cosine, unit, _, _)) in enumerate(zip(pieces, parts)):
        aside = class_grad_aside(share, exponent, cosine, unit, image_facts[at], class_weight)
        grad, loss, embed_part = class_grad_part(images, total, denominator[:, at], *aside, scale, unit)
        if k == 0:
            class_grad, sample_loss, embed_grad = grad, loss, embed_part
        else:
            class_grad = class_grad + grad
    return (sample_loss.reshape(images), embed_grad, class_grad.T)


def solution(mesh):
    placed = (
        P(("dp", "cls"), None),
        P(("dp", "cls"), None),
        P("dp", None),
        P(),
        P(),
        P("dp", None),
        P("cls", None),
        P("dp", "cls", None),
        P("dp", "cls"),
        P("dp"),
    )
    return jax.shard_map(
        per_device,
        mesh=mesh,
        in_specs=placed,
        out_specs=(P(("dp", "cls")), P(("dp", "cls"), None), P("cls", "dp")),
        check_vma=False,
    )
```
